32 devices in a mesh: ctx: 4 (over y, x), exp: 8 (over z, core).
Axes of the slice: x: 2, y: 2, z: 4, core: 2. Of those that a mesh axis runs over, the one named last changes fastest.
Arguments:
- queries: bfloat16 [8, 512, 2048], P('exp', 'ctx'), may hold values from -6 to 6
- key_rows: bfloat16 [8, 512, 256], P('exp', 'ctx'), may hold values from -6 to 6
- value_matrix: bfloat16 [8, 512, 256], P('exp', 'ctx'), may hold values from -4 to 4
- hidden: bfloat16 [8, 512, 2880], P('exp', 'ctx'), may hold values from -30 to 30
- out_weight: bfloat16 [2048, 2880], P('ctx'), may hold values from -0.125 to 0.125
- norm_gain: float32 [2880], replicated, may hold values from 0.1 to 1.9
- block_order: int32 [8], replicated, may hold values from 0 to 7, each once
- expert_ids: int32 [8, 512, 4], P('exp', 'ctx'), may hold values from 0 to 15, all different within a row; in each aligned block of 128 rows (0 to 127, 128 to 255, ..., all dimensions but the last counted through in order) at most 64 rows name the same one
- route_weights: float32 [8, 512, 4], P('exp', 'ctx'), may hold values from 0.1 to 0.6
- gate_up_weight: bfloat16 [32, 2880, 1440], P(('ctx', 'exp')), may hold values from -0.109375 to 0.109375
- down_weight: bfloat16 [32, 720, 2880], P(('ctx', 'exp')), may hold values from -0.15625 to 0.15625
Outputs:
- layer_out: bfloat16 [8, 512, 2880], P('exp', 'ctx')
The draws below stay inside these ranges and needn't reach their ends.
Inputs may be any that keep to these rules, and one draw needn't show every extreme that they name: `expert_ids`: the 128 rows of one device (aligned blocks of rows) name any one expert at most 64 times, a bound that some block reaches.
All inputs are finite; a program needn't handle non-finite values.
Results may differ from the reference program's by a relative error of at most 0.017.
Values may be sent and summed in bfloat16 or wider, within the bound.
No kernel may reach another device: no remote copies, remote signals or barrier semaphores. Data moves between devices by JAX's collectives and lax.ppermute only.
A program may use at most 128 MiB of HBM per device.

```python
import math
import jax
import jax.numpy as jnp
import numpy as np
from jax import lax

D = 2880
QUERY_HEADS = 32
KEY_VALUE_HEADS = 4
HEAD_SIZE = 64
FF = 1440
TOPK = 4
BLK = 64
TOK_DEV = 128
SEQUENCE_LENGTH = 512
FF_HALF = 720
EXPERTS = 16
CAP = 64
N_CTX = 4
N_EXP = 8


def drawn_fields(key):
    base = jax.random.fold_in(key, 11)
    key_layout_shape = (N_EXP, SEQUENCE_LENGTH, KEY_VALUE_HEADS, HEAD_SIZE)
    key_slice_field = jnp.clip(1.5 * jax.random.normal(jax.random.fold_in(base, 1), key_layout_shape, jnp.float32), -6.0, 6.0)
    query_slice_field = jnp.clip(1.5 * jax.random.normal(jax.random.fold_in(base, 2), (N_EXP, SEQUENCE_LENGTH, QUERY_HEADS * HEAD_SIZE), jnp.float32), -6.0, 6.0)
    return (query_slice_field, key_slice_field.reshape(N_EXP, SEQUENCE_LENGTH, KEY_VALUE_HEADS * HEAD_SIZE))


def draw_queries(key, part):
    return drawn_fields(key)[0].astype(jnp.bfloat16)


def draw_key_rows(key, part):
    return drawn_fields(key)[1].astype(jnp.bfloat16)


def draw_hidden(key, part):
    base = jax.random.fold_in(key, 23)
    shape = (N_EXP, SEQUENCE_LENGTH, D)
    field = jnp.clip(jax.random.normal(jax.random.fold_in(base, 1), shape, jnp.float32), -4.0, 4.0)
    row_scale = jnp.exp(jax.random.uniform(jax.random.fold_in(base, 3), (N_EXP, SEQUENCE_LENGTH, 1), jnp.float32, math.log(0.25), math.log(2.5)))
    col_scale = jnp.exp(jax.random.uniform(jax.random.fold_in(base, 4), (1, 1, D), jnp.float32, math.log(0.3), math.log(3.0)))
    return (field * row_scale * col_scale).astype(jnp.bfloat16)


def steps_of(own_key, extent, split, least, top_value):
    def one(axis_at, blocks):
        draws = jax.random.uniform(jax.random.fold_in(jax.random.fold_in(own_key, 6), axis_at), (blocks,), jnp.float32, least / len(split), top_value / len(split))
        return jnp.repeat(jnp.exp(draws), extent[axis_at] // blocks).reshape((-1,) + (1,) * (len(extent) - axis_at - 1))

    factor_of = one(*split[0])
    for cut in split[1:]:
        factor_of = factor_of * one(*cut)
    return factor_of


def routed_block(own_key, own, number, rows, number_of, top, reach, skew):
    ranking = jax.random.permutation(own_key, number_of)
    crowded, ordinary = load_shares(number_of, rows * top, reach, skew, True), load_shares(number_of, rows * top, reach, skew, False)
    places = jnp.arange(number_of)

    def named(tallies, turn):
        used = int((tallies > 0).sum())
        fixed = max(1, used // 4)
        passed = fixed + (places - fixed + turn * (used - fixed)) % max(1, number_of - fixed)
        return jnp.zeros((number_of,), jnp.int32).at[ranking[jnp.where(places < fixed, places, passed)]].set(jnp.asarray(tallies, jnp.int32))

    tallies = jnp.where(number % 4 == 0, named(crowded, number // 4), named(ordinary, number - number // 4 - 1))
    mixed = jax.random.permutation(jax.random.fold_in(own, 3), number_of)
    donor, sink = mixed[0:number_of // 2 * 2:2], mixed[1:number_of // 2 * 2:2]
    slack = jnp.minimum(tallies[donor] - 1, reach - tallies[sink]) // 2
    slack = jnp.where((donor == ranking[0]) | (sink == ranking[0]) | (tallies[sink] == 0), 0, jnp.maximum(slack, 0))
    passed = jax.random.randint(jax.random.fold_in(own, 4), (number_of // 2,), 0, 1 << 20) % (slack + 1)
    tallies = tallies.at[donor].add(-passed).at[sink].add(passed)
    members = jnp.searchsorted(jnp.cumsum(tallies), jnp.arange(rows * top), side="right").astype(jnp.int32)
    listing = members.reshape(top, rows).T
    listing = listing[jax.random.permutation(jax.random.fold_in(own, 1), rows)]
    turn = jax.random.randint(jax.random.fold_in(own, 2), (rows, 1), 0, top)
    return jnp.take_along_axis(listing, (jnp.arange(top)[None, :] + turn) % top, axis=1)


def load_shares(amount, total, most, slope, full):
    portions = [(1 << 20) // math.isqrt(rank ** slope) + 1 for rank in range(1, amount + 1)]
    largest = most if full else min(most, max(-(-total // amount), total * portions[0] // sum(portions)))
    least = 1 if total - largest >= amount - 1 else 0
    counts, rest = [largest] + [least] * (amount - 1), total - largest - least * (amount - 1)
    while rest > 0:
        candidates = [i for i in range(1, amount) if counts[i] < largest] or [i for i in range(1, amount) if counts[i] < most]
        mass, remaining = sum([portions[i] for i in candidates]), rest
        for i in candidates:
            addition = min(most - counts[i], max(1, remaining * portions[i] // mass), rest)
            counts[i] = counts[i] + addition
            rest = rest - addition
    return np.array(counts)


def bell_draw(rng, dims, width, reach, pieces=(), held_as=jnp.bfloat16):
    entries = jax.random.normal(rng, dims, jnp.float32) * width
    if len(pieces) > 0:
        entries = steps_of(rng, dims, pieces, -0.22, 0.18) * entries
    return jnp.clip(entries, min=-reach, max=reach).astype(held_as)


def setup_inputs(seed: int = 0) -> dict:
    splits = jax.random.split(jax.random.key(seed), 12)
    queries = draw_queries(jax.random.fold_in(splits[11], 71), 0)
    key_rows = draw_key_rows(jax.random.fold_in(splits[11], 71), 0)
    value_matrix = bell_draw(splits[2], (N_EXP, SEQUENCE_LENGTH, KEY_VALUE_HEADS * HEAD_SIZE), 1.0, 4.0, ((0, 8), (1, 4)))
    hidden = draw_hidden(jax.random.fold_in(splits[11], 71), 0)
    out_weight = bell_draw(splits[4], (QUERY_HEADS * HEAD_SIZE, D), (QUERY_HEADS * HEAD_SIZE) ** -0.5, 0.125, ((0, 4),))
    norm_gain = jnp.clip(1.0 + 0.18 * jax.random.normal(splits[5], (D,), jnp.float32), 0.1, 1.9)
    block_order = jax.random.permutation(splits[6], 2 * N_CTX).astype(jnp.int32)
    expert_ids_keys = jax.random.split(jax.random.fold_in(splits[7], 1), N_EXP * SEQUENCE_LENGTH // TOK_DEV)
    expert_ids_turns = jax.random.permutation(jax.random.fold_in(splits[7], 3), N_EXP * SEQUENCE_LENGTH // TOK_DEV)
    expert_ids = jax.vmap(lambda own, number: routed_block(jax.random.fold_in(splits[7], 2), own, number, TOK_DEV, EXPERTS, TOPK, CAP, 2))(expert_ids_keys, expert_ids_turns).reshape((N_EXP, SEQUENCE_LENGTH, TOPK))
    route_weights = jnp.clip(0.1 + 0.5 * jax.random.uniform(splits[8], (N_EXP, SEQUENCE_LENGTH, TOPK), jnp.float32) ** steps_of(splits[8], (N_EXP, SEQUENCE_LENGTH, TOPK), ((0, 8), (1, 4)), -0.2, 0.2), 0.1, 0.6)
    gate_up_weight = bell_draw(splits[9], (2 * EXPERTS, D, 2 * FF_HALF), D ** -0.5, 0.109375, ((0, 32),))
    down_weight = bell_draw(splits[10], (2 * EXPERTS, FF_HALF, D), FF ** -0.5, 0.15625, ((0, 32),))
    return dict(queries=queries, key_rows=key_rows, value_matrix=value_matrix, hidden=hidden, out_weight=out_weight, norm_gain=norm_gain, block_order=block_order, expert_ids=expert_ids, route_weights=route_weights, gate_up_weight=gate_up_weight, down_weight=down_weight)


negative_large = -1e+30

def positions_of(block_order):
    row_index = jnp.arange(SEQUENCE_LENGTH, dtype=jnp.int32)
    return block_order[row_index // BLK] * BLK + row_index % BLK

def attend_sequence(query_sequence, key_sequence, value_sequence, positions):
    query_group_size = QUERY_HEADS // KEY_VALUE_HEADS
    query_head_rows = query_sequence.astype(jnp.float32).reshape(SEQUENCE_LENGTH, KEY_VALUE_HEADS, query_group_size, HEAD_SIZE)
    key_head_rows = key_sequence.astype(jnp.float32).reshape(SEQUENCE_LENGTH, KEY_VALUE_HEADS, HEAD_SIZE)
    value_head_rows = value_sequence.astype(jnp.float32).reshape(SEQUENCE_LENGTH, KEY_VALUE_HEADS, HEAD_SIZE)
    scores = jnp.einsum('qhgd,khd->hgqk', query_head_rows, key_head_rows) * HEAD_SIZE ** (-0.5)
    visible = positions[None, :] <= positions[:, None]
    masked = jnp.where(visible, scores, negative_large)
    row_maximum = lax.optimization_barrier(jnp.max(masked, axis=-1, keepdims=True))
    kept_probs = jnp.where(visible, jnp.exp(masked - row_maximum), 0.0)
    row_total = lax.optimization_barrier(jnp.sum(kept_probs, axis=-1))
    probs_low = kept_probs.astype(jnp.bfloat16)
    weighted_sum = jnp.einsum('hgqk,khd->qhgd', probs_low.astype(jnp.float32), value_head_rows)
    attended = weighted_sum / jnp.transpose(row_total, (2, 0, 1))[..., None]
    return attended.reshape(SEQUENCE_LENGTH, QUERY_HEADS * HEAD_SIZE).astype(jnp.bfloat16)

def expert_half(routed, gate_up, down_part):
    gate_up_out = jnp.dot(routed, gate_up, preferred_element_type=jnp.float32)
    gate_part = gate_up_out[:, :FF_HALF]
    up_part = gate_up_out[:, FF_HALF:]
    activated = (gate_part * jax.nn.sigmoid(1.702 * gate_part) * (up_part + 1.0)).astype(jnp.bfloat16)
    return jnp.dot(activated, down_part, preferred_element_type=jnp.float32).astype(jnp.bfloat16)

def reference(queries, key_rows, value_matrix, hidden, out_weight, norm_gain, block_order, expert_ids, route_weights, gate_up_weight, down_weight):
    positions = positions_of(block_order)
    attended = lax.map(lambda triple: attend_sequence(triple[0], triple[1], triple[2], positions), (queries, key_rows, value_matrix))
    projected = jnp.dot(attended.reshape(-1, QUERY_HEADS * HEAD_SIZE), out_weight, preferred_element_type=jnp.float32)
    residual = (hidden.reshape(-1, D).astype(jnp.float32) + projected).astype(jnp.bfloat16)
    res_float = residual.astype(jnp.float32)
    moe_in = (res_float * lax.rsqrt(lax.optimization_barrier(jnp.mean(res_float * res_float, axis=-1, keepdims=True)) + 1e-05) * norm_gain).astype(jnp.bfloat16)
    flat_ids = expert_ids.reshape(-1)
    flat_weights = route_weights.reshape(-1)
    limit = N_EXP * N_CTX * CAP

    def one_expert(moe_total, expert):
        matches = flat_ids == expert
        picked = jnp.nonzero(matches, size=limit, fill_value=0)[0].astype(jnp.int32)
        is_valid = jnp.arange(limit, dtype=jnp.int32) < jnp.sum(matches.astype(jnp.int32))
        tokens = picked // TOPK
        weights_now = jnp.where(is_valid, flat_weights[picked], 0.0)
        routed = moe_in[tokens]
        first_half = expert_half(routed, gate_up_weight[2 * expert], down_weight[2 * expert]).astype(jnp.float32)
        second_half = expert_half(routed, gate_up_weight[2 * expert + 1], down_weight[2 * expert + 1]).astype(jnp.float32)
        combined = (first_half + second_half).astype(jnp.bfloat16).astype(jnp.float32)
        return (moe_total.at[tokens].add(weights_now[:, None] * combined), None)
    moe_total, _ = lax.scan(one_expert, jnp.zeros((N_EXP * SEQUENCE_LENGTH, D), jnp.float32), jnp.arange(EXPERTS, dtype=jnp.int32))
    return (res_float + moe_total).astype(jnp.bfloat16).reshape(N_EXP, SEQUENCE_LENGTH, D)
```

```python
import jax
import jax.numpy as jnp
from jax import lax
from jax.sharding import PartitionSpec as P

D = 2880
QUERY_HEADS = 32
KEY_VALUE_HEADS = 4
HEAD_SIZE = 64
TOPK = 4


negative_large = -1e30


def ctx_swap(rows, distance):
    if distance == 0:
        return rows
    count = lax.axis_size("ctx")
    return lax.ppermute(rows, "ctx", [(i, i ^ distance) for i in range(count)])


def plane_shift(rows, planes):
    count = lax.axis_size("exp")
    if (2 * planes) % count == 0:
        return rows
    return lax.ppermute(rows, "exp", [(i, (i + 2 * planes) % count) for i in range(count)])


def core_swap(rows):
    count = lax.axis_size("exp")
    return lax.ppermute(rows, "exp", [(i, i ^ 1) for i in range(count)])


def activate(routed, gate_up):
    half_size = gate_up.shape[1] // 2
    gate_up_out = jnp.dot(routed, gate_up, preferred_element_type=jnp.float32)
    gate_part = gate_up_out[:, :half_size]
    up_part = gate_up_out[:, half_size:]
    return (gate_part * jax.nn.sigmoid(1.702 * gate_part) * (up_part + 1.0)).astype(jnp.bfloat16)


def attend(queries, keys, values, query_pos, key_pos):
    scores = jnp.einsum("qgd,kd->gqk", queries, keys, preferred_element_type=jnp.float32)
    scores = scores * HEAD_SIZE ** (-0.5)
    visible = key_pos[None, :] <= query_pos[:, None]
    masked = jnp.where(visible, scores, negative_large)
    row_maximum = jnp.max(masked, axis=-1, keepdims=True)
    kept_probs = jnp.where(visible, jnp.exp(masked - row_maximum), 0.0)
    row_total = jnp.sum(kept_probs, axis=-1)
    weighted_sum = jnp.einsum(
        "gqk,kd->qgd", kept_probs.astype(jnp.bfloat16), values, preferred_element_type=jnp.float32
    )
    attended = weighted_sum / jnp.transpose(row_total)[..., None]
    return attended.astype(jnp.bfloat16).reshape(queries.shape[0], -1)


def local(
    queries,
    key_rows,
    value_matrix,
    hidden,
    out_weight,
    norm_gain,
    block_order,
    expert_ids,
    route_weights,
    gate_up_weight,
    down_weight,
):
    ctx_count = lax.axis_size("ctx")
    exp_count = lax.axis_size("exp")
    planes = exp_count // 2
    ctx_index = lax.axis_index("ctx")
    plane_index = lax.axis_index("exp") // 2
    token_count = queries.shape[1]
    block_len = token_count // 2
    experts = ctx_count * planes
    capacity = 2 * token_count * TOPK // experts
    heads_here = QUERY_HEADS // ctx_count
    group = QUERY_HEADS // KEY_VALUE_HEADS
    slot_ids = jnp.arange(2 * ctx_count, dtype=jnp.int32)

    gate_up_mine, down_mine = gate_up_weight[0], down_weight[0]
    gate_up_other, down_other = core_swap(gate_up_mine), core_swap(down_mine)

    routing = jnp.concatenate(
        [expert_ids[0].astype(jnp.float32), route_weights[0]], axis=1
    ).T
    routing = jnp.stack([plane_shift(routing, s) for s in range(planes)])
    ids, weights = routing[:, None, :TOPK], routing[:, None, TOPK:]
    partner = ctx_index ^ jnp.arange(ctx_count, dtype=jnp.int32)
    wanted = (partner * planes + plane_index).astype(jnp.float32)
    chosen = ids == wanted[None, :, None, None]
    member = jnp.any(chosen, axis=2)
    weight_of = jnp.sum(jnp.where(chosen, weights, 0.0), axis=2)
    token_ids = jnp.arange(token_count, dtype=jnp.int32)
    before = (token_ids[:, None] < token_ids[None, :]).astype(jnp.bfloat16)
    rank = jnp.einsum(
        "sct,tu->scu", member.astype(jnp.bfloat16), before, preferred_element_type=jnp.float32
    )
    slots = jnp.arange(capacity, dtype=jnp.float32)
    placed = (rank[:, :, None, :] == slots[None, None, :, None]) & member[:, :, None, :]
    pick = placed.astype(jnp.bfloat16)
    mix = jnp.where(placed, weight_of[:, :, None, :], 0.0).astype(jnp.bfloat16)

    def locate(row_index):
        table = (row_index // block_len)[:, None] == slot_ids[None, :]
        return (
            jnp.sum(jnp.where(table, block_order[None, :], 0), axis=1) * block_len
            + row_index % block_len
        )

    def for_partner(d):
        to = ctx_index ^ d
        first = to * heads_here
        kv_first = (first // group) * HEAD_SIZE
        return jnp.concatenate(
            [
                lax.dynamic_slice_in_dim(queries[0], first * HEAD_SIZE, heads_here * HEAD_SIZE, 1),
                lax.dynamic_slice_in_dim(key_rows[0], kv_first, HEAD_SIZE, 1),
                lax.dynamic_slice_in_dim(value_matrix[0], kv_first, HEAD_SIZE, 1),
            ],
            axis=1,
        )

    got = [ctx_swap(for_partner(d), d) for d in range(ctx_count)]
    width = heads_here * HEAD_SIZE
    keys = jnp.concatenate([g[:, width : width + HEAD_SIZE] for g in got])
    values = jnp.concatenate([g[:, width + HEAD_SIZE :] for g in got])
    places = [locate((ctx_index ^ d) * token_count + token_ids) for d in range(ctx_count)]
    key_pos = jnp.concatenate(places)
    projected = []
    for d in range(ctx_count):
        attended = attend(
            got[d][:, :width].reshape(token_count, heads_here, HEAD_SIZE),
            keys,
            values,
            places[d],
            key_pos,
        )
        part = jnp.dot(attended, out_weight, preferred_element_type=jnp.float32)
        projected.append(part if d == 0 else ctx_swap(part.astype(jnp.bfloat16), d))
    total = hidden[0].astype(jnp.float32) + projected[0]
    for part in projected[1:]:
        total = total + part.astype(jnp.float32)
    residual = total.astype(jnp.bfloat16)
    res_float = residual.astype(jnp.float32)
    moe_in = (
        res_float
        * lax.rsqrt(jnp.mean(res_float * res_float, axis=-1, keepdims=True) + 1e-05)
        * norm_gain
    ).astype(jnp.bfloat16)

    held = moe_in
    out = res_float
    for s in range(planes):
        if s > 0:
            held = plane_shift(held, 1)
        arrived = []
        for d in range(ctx_count):
            rows = jnp.dot(pick[s, d], held, preferred_element_type=jnp.float32)
            arrived.append(ctx_swap(rows.astype(jnp.bfloat16), d))
        routed = jnp.concatenate(arrived)
        result = jnp.dot(
            activate(routed, gate_up_mine), down_mine, preferred_element_type=jnp.float32
        ) + jnp.dot(
            activate(routed, gate_up_other), down_other, preferred_element_type=jnp.float32
        )
        result = result.astype(jnp.bfloat16).reshape(ctx_count, capacity, D)
        returned = jnp.concatenate([ctx_swap(result[d], d) for d in range(ctx_count)])
        mixed = jnp.einsum(
            "rt,rd->td",
            mix[s].reshape(ctx_count * capacity, token_count),
            returned,
            preferred_element_type=jnp.float32,
        )
        if s == 0:
            out = out + mixed
        else:
            out = out + plane_shift(mixed.astype(jnp.bfloat16), -s).astype(jnp.float32)
    return out.astype(jnp.bfloat16)[None]


def solution(mesh):
    return jax.shard_map(
        local,
        mesh=mesh,
        in_specs=(
            P("exp", "ctx", None),
            P("exp", "ctx", None),
            P("exp", "ctx", None),
            P("exp", "ctx", None),
            P("ctx", None),
            P(),
            P(),
            P("exp", "ctx", None),
            P("exp", "ctx", None),
            P(("ctx", "exp"), None, None),
            P(("ctx", "exp"), None, None),
        ),
        out_specs=P("exp", "ctx", None),
        check_vma=False,
    )
```

```python
import functools

import jax
import jax.numpy as jnp
from jax import lax
from jax.experimental import pallas as pl
from jax.experimental.pallas import tpu as pltpu
from jax.sharding import PartitionSpec as P

D = 2880
QUERY_HEADS = 32
KEY_VALUE_HEADS = 4
HEAD_SIZE = 64
TOPK = 4


negative_large = -1e30


def ctx_swap(rows, distance):
    if distance == 0:
        return rows
    count = lax.axis_size("ctx")
    return lax.ppermute(rows, "ctx", [(i, i ^ distance) for i in range(count)])


def plane_shift(rows, planes):
    count = lax.axis_size("exp")
    if (2 * planes) % count == 0:
        return rows
    return lax.ppermute(rows, "exp", [(i, (i + 2 * planes) % count) for i in range(count)])


def core_swap(rows):
    count = lax.axis_size("exp")
    return lax.ppermute(rows, "exp", [(i, i ^ 1) for i in range(count)])


def vmem(shape_list):
    return [pl.BlockSpec(memory_space=pltpu.VMEM)] * len(shape_list)


SMEM_SPEC = pl.BlockSpec(memory_space=pltpu.SMEM)


def nt_dot(left, right):
    return lax.dot_general(
        left, right, (((1,), (1,)), ((), ())), preferred_element_type=jnp.float32
    )


def pack_kernel(ctx_count, ctx_ref, q_ref, k_ref, v_ref, *out_refs):
    heads_here = QUERY_HEADS // ctx_count
    group = QUERY_HEADS // KEY_VALUE_HEADS
    width = heads_here * HEAD_SIZE
    rows = q_ref.shape[0]
    low = lax.broadcasted_iota(jnp.int32, (rows, 2 * HEAD_SIZE), 1) < HEAD_SIZE
    for d in range(ctx_count):
        to = ctx_ref[0] ^ d
        head = (to * heads_here) // group
        odd = (head % 2) == 1
        pair = pl.ds(pl.multiple_of((head // 2) * 2 * HEAD_SIZE, 2 * HEAD_SIZE), 2 * HEAD_SIZE)
        keys = k_ref[:, pair].astype(jnp.float32)
        values = v_ref[:, pair].astype(jnp.float32)
        keys = jnp.where(odd, pltpu.roll(keys, HEAD_SIZE, 1), keys)
        values = jnp.where(odd, values, pltpu.roll(values, HEAD_SIZE, 1))
        columns = pl.ds(pl.multiple_of(to * width, width), width)
        scaled = q_ref[:, columns].astype(jnp.float32) * HEAD_SIZE ** (-0.5)
        out_refs[d][:, :width] = scaled.astype(jnp.bfloat16)
        out_refs[d][:, width:] = jnp.where(low, keys, values).astype(jnp.bfloat16)


def pack(ctx_scalar, queries, keys, values, ctx_count):
    rows, width = queries.shape[0], queries.shape[1] // ctx_count
    shape = jax.ShapeDtypeStruct((rows, width + 2 * HEAD_SIZE), jnp.bfloat16)
    return pl.pallas_call(
        functools.partial(pack_kernel, ctx_count),
        out_shape=[shape] * ctx_count,
        in_specs=[SMEM_SPEC] + vmem([0] * 3),
        out_specs=vmem([0] * ctx_count),
        compiler_params=pltpu.CompilerParams(vmem_limit_bytes=8 << 20),
        cost_estimate=pl.CostEstimate(flops=0, bytes_accessed=4 << 20, transcendentals=0),
    )(ctx_scalar, queries, keys, values)


def attend_kernel(dests, ctx_count, ctx_ref, order_ref, weight_ref, *refs):
    got_refs, out_refs = refs[:ctx_count], refs[ctx_count:]
    heads_here = QUERY_HEADS // ctx_count
    width = heads_here * HEAD_SIZE
    rows = got_refs[0].shape[0]
    block = rows // 2
    me = ctx_ref[0]
    lanes = lax.broadcasted_iota(jnp.int32, (rows, 2 * HEAD_SIZE), 1) < HEAD_SIZE
    keys, values, key_pos = [], [], []
    place = lax.broadcasted_iota(jnp.int32, (1, rows), 1)
    for d in range(ctx_count):
        both = got_refs[d][:, width:].astype(jnp.float32)
        other = pltpu.roll(both, HEAD_SIZE, 1)
        keys.append(jnp.where(lanes, both, other).astype(jnp.bfloat16))
        values.append(jnp.where(lanes, other, both).astype(jnp.bfloat16))
        slot = 2 * (me ^ d)
        first, second = order_ref[slot] * block, order_ref[slot + 1] * block - block
        key_pos.append(place + jnp.where(place < block, first, second))
    keys = jnp.concatenate(keys, axis=0)
    values = jnp.concatenate(values, axis=0)
    key_pos = jnp.concatenate(key_pos, axis=1)
    row = lax.broadcasted_iota(jnp.int32, (rows, 1), 0)
    for out_ref, d in zip(out_refs, dests):
        slot = 2 * (me ^ d)
        first, second = order_ref[slot] * block, order_ref[slot + 1] * block - block
        query_pos = row + jnp.where(row < block, first, second)
        visible = key_pos <= query_pos
        attended = []
        for pair in range(heads_here // 2):
            both = got_refs[d][:, pair * 2 * HEAD_SIZE : (pair + 1) * 2 * HEAD_SIZE]
            sides = []
            for side in range(2):
                query = jnp.where(lanes == (side == 0), both, jnp.zeros_like(both))
                scores = jnp.where(visible, nt_dot(query, keys), negative_large)
                probs = jnp.exp(scores - jnp.max(scores, axis=-1, keepdims=True))
                total = jnp.sum(probs, axis=-1, keepdims=True)
                mixed = jnp.dot(
                    probs.astype(jnp.bfloat16), values, preferred_element_type=jnp.float32
                )
                sides.append(mixed / total)
            attended.append(jnp.where(lanes, sides[0], sides[1]).astype(jnp.bfloat16))
        attended = jnp.concatenate(attended, axis=1)
        out_ref[...] = nt_dot(attended, weight_ref[...]).astype(out_ref.dtype)


def attend(dests, ctx_scalar, order, weight, got, dtype):
    ctx_count = len(got)
    rows = got[0].shape[0]
    shape = jax.ShapeDtypeStruct((rows, weight.shape[0]), dtype)
    work = len(dests) * rows * weight.shape[1]
    return pl.pallas_call(
        functools.partial(attend_kernel, dests, ctx_count),
        out_shape=[shape] * len(dests),
        in_specs=[SMEM_SPEC, SMEM_SPEC] + vmem([0] * (1 + ctx_count)),
        out_specs=vmem(dests),
        compiler_params=pltpu.CompilerParams(vmem_limit_bytes=24 << 20),
        cost_estimate=pl.CostEstimate(
            flops=2 * work * (weight.shape[0] + 2 * ctx_count * rows),
            bytes_accessed=8 << 20,
            transcendentals=work * ctx_count * rows // HEAD_SIZE,
        ),
    )(ctx_scalar, order, weight, *got)


def norm_kernel(part_count, hidden_ref, gain_ref, pick_ref, *refs):
    part_refs, (residual_ref, normed_ref, *out_refs) = refs[:part_count], refs[part_count:]
    total = hidden_ref[...].astype(jnp.float32)
    for part_ref in part_refs:
        total = total + part_ref[...].astype(jnp.float32)
    residual = total.astype(jnp.bfloat16)
    residual_ref[...] = residual
    res_float = residual.astype(jnp.float32)
    mean = jnp.mean(res_float * res_float, axis=-1, keepdims=True)
    normed = (res_float * lax.rsqrt(mean + 1e-05) * gain_ref[...]).astype(jnp.bfloat16)
    normed_ref[...] = normed
    for d, out_ref in enumerate(out_refs):
        out_ref[...] = jnp.dot(
            pick_ref[d], normed, preferred_element_type=jnp.float32
        ).astype(jnp.bfloat16)


def norm_and_pick(hidden, gain, pick, parts):
    rows, columns = hidden.shape
    ctx_count, capacity, _ = pick.shape
    whole = jax.ShapeDtypeStruct((rows, columns), jnp.bfloat16)
    slot = jax.ShapeDtypeStruct((capacity, columns), jnp.bfloat16)
    return pl.pallas_call(
        functools.partial(norm_kernel, len(parts)),
        out_shape=[whole, whole] + [slot] * ctx_count,
        in_specs=vmem([0] * (3 + len(parts))),
        out_specs=vmem([0] * (2 + ctx_count)),
        compiler_params=pltpu.CompilerParams(vmem_limit_bytes=24 << 20),
        cost_estimate=pl.CostEstimate(
            flops=2 * ctx_count * capacity * rows * columns,
            bytes_accessed=6 << 20,
            transcendentals=rows,
        ),
    )(hidden, gain, pick, *parts)


def pick_kernel(pick_ref, held_ref, *out_refs):
    for d, out_ref in enumerate(out_refs):
        out_ref[...] = jnp.dot(
            pick_ref[d], held_ref[...], preferred_element_type=jnp.float32
        ).astype(jnp.bfloat16)


def pick_rows(pick, held):
    rows, columns = held.shape
    ctx_count, capacity, _ = pick.shape
    slot = jax.ShapeDtypeStruct((capacity, columns), jnp.bfloat16)
    return pl.pallas_call(
        pick_kernel,
        out_shape=[slot] * ctx_count,
        in_specs=vmem([0] * 2),
        out_specs=vmem([0] * ctx_count),
        compiler_params=pltpu.CompilerParams(vmem_limit_bytes=16 << 20),
        cost_estimate=pl.CostEstimate(
            flops=2 * ctx_count * capacity * rows * columns,
            bytes_accessed=3 << 20,
            transcendentals=0,
        ),
    )(pick, held)


def expert_kernel(ctx_count, steps, *refs):
    row_refs = refs[:ctx_count]
    gate_up_refs, down_refs = refs[ctx_count : ctx_count + 2], refs[ctx_count + 2 : ctx_count + 4]
    out_refs = refs[ctx_count + 4 : 2 * ctx_count + 4]
    routed_ref, total_ref = refs[2 * ctx_count + 4 :]
    capacity = row_refs[0].shape[0]
    step = pl.program_id(0)

    @pl.when(step == 0)
    def _():
        for d in range(ctx_count):
            routed_ref[d * capacity : (d + 1) * capacity, :] = row_refs[d][...]

    routed = routed_ref[...]
    added = None
    for gate_up_ref, down_ref in zip(gate_up_refs, down_refs):
        gate = nt_dot(routed, gate_up_ref[0])
        up = nt_dot(routed, gate_up_ref[1])
        activated = (gate * jax.nn.sigmoid(1.702 * gate) * (up + 1.0)).astype(jnp.bfloat16)
        term = jnp.dot(activated, down_ref[...], preferred_element_type=jnp.float32)
        added = term if added is None else added + term

    @pl.when(step == 0)
    def _():
        total_ref[...] = added

    @pl.when((step > 0) & (step < steps - 1))
    def _():
        total_ref[...] += added

    @pl.when(step == steps - 1)
    def _():
        result = (total_ref[...] + added).astype(jnp.bfloat16)
        for d in range(ctx_count):
            out_refs[d][...] = result[d * capacity : (d + 1) * capacity]


def expert(rows, gate_ups, downs):
    ctx_count = len(rows)
    capacity, columns = rows[0].shape
    half = downs[0].shape[0]
    steps = 3
    tile = half // steps
    count = ctx_count * capacity
    fixed = pl.BlockSpec((capacity, columns), lambda i: (0, 0))
    return pl.pallas_call(
        functools.partial(expert_kernel, ctx_count, steps),
        grid=(steps,),
        out_shape=[jax.ShapeDtypeStruct((capacity, columns), jnp.bfloat16)] * ctx_count,
        in_specs=[fixed] * ctx_count
        + [pl.BlockSpec((2, tile, columns), lambda i: (0, i, 0))] * 2
        + [pl.BlockSpec((tile, columns), lambda i: (i, 0))] * 2,
        out_specs=[fixed] * ctx_count,
        scratch_shapes=[
            pltpu.VMEM((count, columns), jnp.bfloat16),
            pltpu.VMEM((count, columns), jnp.float32),
        ],
        compiler_params=pltpu.CompilerParams(vmem_limit_bytes=44 << 20),
        cost_estimate=pl.CostEstimate(
            flops=12 * count * columns * half,
            bytes_accessed=12 * half * columns,
            transcendentals=2 * count * half,
        ),
    )(*rows, *gate_ups, *downs)


def mix_kernel(ctx_count, mix_ref, *refs):
    back_refs, extra_refs, out_ref = refs[:ctx_count], refs[ctx_count:-1], refs[-1]
    back = jnp.concatenate([ref[...] for ref in back_refs], axis=0)
    total = jnp.dot(mix_ref[...], back, preferred_element_type=jnp.float32)
    for ref in extra_refs:
        total = total + ref[...].astype(jnp.float32)
    out_ref[...] = total.astype(jnp.bfloat16)


def mix_rows(mix, back, extra):
    tokens, count = mix.shape
    columns = back[0].shape[1]
    return pl.pallas_call(
        functools.partial(mix_kernel, len(back)),
        out_shape=jax.ShapeDtypeStruct((tokens, columns), jnp.bfloat16),
        in_specs=vmem([0] * (1 + len(back) + len(extra))),
        out_specs=pl.BlockSpec(memory_space=pltpu.VMEM),
        compiler_params=pltpu.CompilerParams(vmem_limit_bytes=24 << 20),
        cost_estimate=pl.CostEstimate(
            flops=2 * count * tokens * columns,
            bytes_accessed=2 * columns * (count + tokens * (1 + len(extra))),
            transcendentals=0,
        ),
    )(mix, *back, *extra)


def local(
    queries,
    key_rows,
    value_matrix,
    hidden,
    out_weight,
    norm_gain,
    block_order,
    expert_ids,
    route_weights,
    gate_up_weight,
    down_weight,
):
    ctx_count = lax.axis_size("ctx")
    exp_count = lax.axis_size("exp")
    planes = exp_count // 2
    ctx_index = lax.axis_index("ctx")
    plane_index = lax.axis_index("exp") // 2
    token_count = queries.shape[1]
    experts = ctx_count * planes
    capacity = 2 * token_count * TOPK // experts

    gate_up_mine = jnp.swapaxes(gate_up_weight[0], 0, 1)
    down_mine = down_weight[0]
    half = down_mine.shape[0]
    gate_ups = [gate_up_mine.reshape(2, half, D), core_swap(gate_up_mine).reshape(2, half, D)]
    downs = [down_mine, core_swap(down_mine)]

    routing = jnp.concatenate(
        [expert_ids[0].astype(jnp.float32), route_weights[0]], axis=1
    ).T
    routing = jnp.stack([plane_shift(routing, s) for s in range(planes)])
    ids, weights = routing[:, None, :TOPK], routing[:, None, TOPK:]
    partner = ctx_index ^ jnp.arange(ctx_count, dtype=jnp.int32)
    wanted = (partner * planes + plane_index).astype(jnp.float32)
    chosen = ids == wanted[None, :, None, None]
    member = jnp.any(chosen, axis=2)
    weight_of = jnp.sum(jnp.where(chosen, weights, 0.0), axis=2)
    token_ids = jnp.arange(token_count, dtype=jnp.int32)
    before = (token_ids[:, None] < token_ids[None, :]).astype(jnp.bfloat16)
    rank = jnp.einsum(
        "sct,tu->scu", member.astype(jnp.bfloat16), before, preferred_element_type=jnp.float32
    )
    slots = jnp.arange(capacity, dtype=jnp.float32)
    placed = (rank[:, :, None, :] == slots[None, None, :, None]) & member[:, :, None, :]
    pick = placed.astype(jnp.bfloat16)
    mix = jnp.where(placed, weight_of[:, :, None, :], 0.0).astype(jnp.bfloat16)

    mix = jnp.swapaxes(mix.reshape(planes, ctx_count * capacity, token_count), 1, 2)

    ctx_scalar = ctx_index.astype(jnp.int32).reshape(1)
    packed = pack(ctx_scalar, queries[0], key_rows[0], value_matrix[0], ctx_count)
    got = [ctx_swap(packed[d], d) for d in range(ctx_count)]
    weight = jnp.swapaxes(out_weight, 0, 1)
    parts = []
    for d in range(ctx_count - 1, -1, -1):
        dtype = jnp.bfloat16 if d else jnp.float32
        (part,) = attend((d,), ctx_scalar, block_order, weight, got, dtype)
        parts.append(ctx_swap(part, d))
    residual, held, *rows = norm_and_pick(hidden[0], norm_gain[None], pick[0], parts)

    extra = [residual]
    for s in range(planes):
        if s > 0:
            held = plane_shift(held, 1)
            rows = pick_rows(pick[s], held)
        arrived = [ctx_swap(rows[d], d) for d in range(ctx_count)]
        result = expert(arrived, gate_ups, downs)
        back = [ctx_swap(result[d], d) for d in range(ctx_count)]
        if s == 0:
            own_back = back
        else:
            extra.append(plane_shift(mix_rows(mix[s], back, []), -s))
    return mix_rows(mix[0], own_back, extra)[None]


def solution(mesh):
    return jax.shard_map(
        local,
        mesh=mesh,
        in_specs=(
            P("exp", "ctx", None),
            P("exp", "ctx", None),
            P("exp", "ctx", None),
            P("exp", "ctx", None),
            P("ctx", None),
            P(),
            P(),
            P("exp", "ctx", None),
            P("exp", "ctx", None),
            P(("ctx", "exp"), None, None),
            P(("ctx", "exp"), None, None),
        ),
        out_specs=P("exp", "ctx", None),
        check_vma=False,
    )
```

```python
import functools

import jax
import jax.numpy as jnp
from jax import lax
from jax.experimental import pallas as pl
from jax.experimental.pallas import tpu as pltpu
from jax.sharding import PartitionSpec as P

D = 2880
QUERY_HEADS = 32
KEY_VALUE_HEADS = 4
HEAD_SIZE = 64
TOPK = 4


negative_large = -1e30


def ctx_swap(rows, distance):
    if distance == 0:
        return rows
    count = lax.axis_size("ctx")
    return lax.ppermute(rows, "ctx", [(i, i ^ distance) for i in range(count)])


def plane_shift(rows, planes):
    count = lax.axis_size("exp")
    if (2 * planes) % count == 0:
        return rows
    return lax.ppermute(rows, "exp", [(i, (i + 2 * planes) % count) for i in range(count)])


def core_swap(rows):
    count = lax.axis_size("exp")
    return lax.ppermute(rows, "exp", [(i, i ^ 1) for i in range(count)])

ANY_SPEC = pl.BlockSpec(memory_space=pl.ANY)
SMEM_SPEC = pl.BlockSpec(memory_space=pltpu.SMEM)
VMEM_SPEC = pl.BlockSpec(memory_space=pltpu.VMEM)
SMALL_COST = pl.CostEstimate(flops=1, bytes_accessed=1, transcendentals=0)


def nt_dot(left, right):
    return lax.dot_general(
        left, right, (((1,), (1,)), ((), ())), preferred_element_type=jnp.float32
    )


def nn_dot(left, right):
    return jnp.dot(left, right, preferred_element_type=jnp.float32)


def merged(block):
    return block.reshape(block.shape[0] * block.shape[1], block.shape[2])


def pack_kernel(ctx_count, ctx_ref, q_ref, k_ref, v_ref, *out_refs):
    heads_here = QUERY_HEADS // ctx_count
    group = QUERY_HEADS // KEY_VALUE_HEADS
    width = heads_here * HEAD_SIZE
    rows = q_ref.shape[0]
    low = lax.broadcasted_iota(jnp.int32, (rows, 2 * HEAD_SIZE), 1) < HEAD_SIZE
    for d in range(ctx_count):
        to = ctx_ref[0] ^ d
        head = (to * heads_here) // group
        odd = (head % 2) == 1
        pair = pl.ds(pl.multiple_of((head // 2) * 2 * HEAD_SIZE, 2 * HEAD_SIZE), 2 * HEAD_SIZE)
        keys = k_ref[:, pair].astype(jnp.float32)
        values = v_ref[:, pair].astype(jnp.float32)
        keys = jnp.where(odd, pltpu.roll(keys, HEAD_SIZE, 1), keys)
        values = jnp.where(odd, values, pltpu.roll(values, HEAD_SIZE, 1))
        columns = pl.ds(pl.multiple_of(to * width, width), width)
        out_refs[d][:, :width] = q_ref[:, columns]
        out_refs[d][:, width:] = jnp.where(low, keys, values).astype(jnp.bfloat16)


def pack(ctx_scalar, queries, keys, values, ctx_count):
    rows, width = queries.shape[0], queries.shape[1] // ctx_count
    shape = jax.ShapeDtypeStruct((rows, width + 2 * HEAD_SIZE), jnp.bfloat16)
    return pl.pallas_call(
        functools.partial(pack_kernel, ctx_count),
        out_shape=[shape] * ctx_count,
        in_specs=[SMEM_SPEC] + [VMEM_SPEC] * 3,
        out_specs=[VMEM_SPEC] * ctx_count,
        compiler_params=pltpu.CompilerParams(vmem_limit_bytes=4 << 20),
        cost_estimate=SMALL_COST,
    )(ctx_scalar, queries, keys, values)


def copy_kernel(source_ref, *refs):
    refs[-1][...] = source_ref[...]


def copy_after(source, after):
    return pl.pallas_call(
        copy_kernel,
        out_shape=jax.ShapeDtypeStruct(source.shape, source.dtype),
        in_specs=[VMEM_SPEC] + [ANY_SPEC] * len(after),
        out_specs=VMEM_SPEC,
        compiler_params=pltpu.CompilerParams(vmem_limit_bytes=20 << 20),
        cost_estimate=SMALL_COST,
    )(source, *after)


def attend_kernel(dests, ctx_count, ctx_ref, order_ref, weight_ref, *refs):
    got_refs, hidden_ref, out_refs = refs[:ctx_count], refs[ctx_count], refs[-len(dests) :]
    heads_here = QUERY_HEADS // ctx_count
    width = heads_here * HEAD_SIZE
    rows = got_refs[0].shape[0]
    block = rows // 2
    me = ctx_ref[0]
    lanes = lax.broadcasted_iota(jnp.int32, (rows, 2 * HEAD_SIZE), 1) < HEAD_SIZE
    keys, values, key_pos = [], [], []
    place = lax.broadcasted_iota(jnp.int32, (1, rows), 1)
    for d in range(ctx_count):
        both = got_refs[d][:, width:].astype(jnp.float32)
        other = pltpu.roll(both, HEAD_SIZE, 1)
        scaled = jnp.where(lanes, both, other) * HEAD_SIZE ** (-0.5)
        keys.append(scaled.astype(jnp.bfloat16))
        values.append(jnp.where(lanes, other, both).astype(jnp.bfloat16))
        slot = 2 * (me ^ d)
        first, second = order_ref[slot] * block, order_ref[slot + 1] * block - block
        key_pos.append(place + jnp.where(place < block, first, second))
    keys = jnp.concatenate(keys, axis=0)
    values = jnp.concatenate(values, axis=0)
    key_pos = jnp.concatenate(key_pos, axis=1)
    row = lax.broadcasted_iota(jnp.int32, (rows, 1), 0)
    for out_ref, d in zip(out_refs, dests):
        slot = 2 * (me ^ d)
        first, second = order_ref[slot] * block, order_ref[slot + 1] * block - block
        query_pos = row + jnp.where(row < block, first, second)
        visible = jnp.concatenate([key_pos <= query_pos] * heads_here, axis=0)
        stacked = []
        for pair in range(heads_here // 2):
            both = got_refs[d][:, pair * 2 * HEAD_SIZE : (pair + 1) * 2 * HEAD_SIZE]
            for side in range(2):
                stacked.append(jnp.where(lanes == (side == 0), both, jnp.zeros_like(both)))
        scores = nt_dot(jnp.concatenate(stacked, axis=0), keys)
        scores = jnp.where(visible, scores, negative_large)
        probs = jnp.exp(scores - jnp.max(scores, axis=-1, keepdims=True))
        total = jnp.sum(probs, axis=-1, keepdims=True)
        mixed = nn_dot(probs.astype(jnp.bfloat16), values) / total
        attended = []
        for pair in range(heads_here // 2):
            sides = [mixed[(2 * pair + i) * rows : (2 * pair + i + 1) * rows] for i in range(2)]
            attended.append(jnp.where(lanes, sides[0], sides[1]).astype(jnp.bfloat16))
        part = nt_dot(jnp.concatenate(attended, axis=1), weight_ref[...])
        if d == 0:
            eye = lax.broadcasted_iota(jnp.int32, (rows, rows), 1) == row
            part = part + nt_dot(eye.astype(jnp.bfloat16), hidden_ref[...])
        out_ref[...] = part.astype(out_ref.dtype).reshape(out_ref.shape)


def attend(dests, ctx_scalar, order, weight, got, hidden, after):
    ctx_count = len(got)
    rows, columns = got[0].shape[0], weight.shape[0]
    shapes = [
        jax.ShapeDtypeStruct((2, rows // 2, columns), jnp.bfloat16 if d else jnp.float32)
        for d in dests
    ]
    extra = [hidden] if 0 in dests else []
    work = len(dests) * rows * weight.shape[1]
    return pl.pallas_call(
        functools.partial(attend_kernel, dests, ctx_count),
        out_shape=shapes,
        in_specs=[SMEM_SPEC, SMEM_SPEC]
        + [VMEM_SPEC] * (1 + ctx_count + len(extra))
        + [ANY_SPEC] * len(after),
        out_specs=[VMEM_SPEC] * len(dests),
        compiler_params=pltpu.CompilerParams(vmem_limit_bytes=20 << 20),
        cost_estimate=SMALL_COST,
    )(ctx_scalar, order, weight, *got, *extra, *after)


def pick_and_mix(ctx_count, capacity, ctx_ref, plane_ref, held, route, out_refs, mix_ref):
    tokens = held.shape[0]
    count = ctx_count * capacity
    lane = lax.broadcasted_iota(jnp.int32, (1, count), 1)
    partner = ctx_ref[0] ^ (lane // capacity)
    wanted = (partner * plane_ref[1] + plane_ref[0]).astype(jnp.float32)
    member = jnp.zeros((tokens, count), jnp.float32)
    weight = jnp.zeros((tokens, count), jnp.float32)
    for k in range(TOPK):
        chosen = route[:, k : k + 1] == wanted
        member = jnp.where(chosen, 1.0, member)
        weight = jnp.where(chosen, route[:, TOPK + k : TOPK + k + 1], weight)
    row = lax.broadcasted_iota(jnp.int32, (tokens, tokens), 0)
    earlier = lax.broadcasted_iota(jnp.int32, (tokens, tokens), 1) < row
    rank = nn_dot(earlier.astype(jnp.bfloat16), member.astype(jnp.bfloat16))
    slot = (lane % capacity).astype(jnp.float32)
    placed = jnp.where(rank == slot, member, 0.0)
    mix_ref[...] = (placed * weight).astype(jnp.bfloat16)
    picked = nn_dot(placed.T.astype(jnp.bfloat16), held).astype(jnp.bfloat16)
    for d, out_ref in enumerate(out_refs):
        out_ref[...] = picked[d * capacity : (d + 1) * capacity]


def norm_kernel(part_count, ctx_ref, plane_ref, gain_ref, route_ref, *refs):
    part_refs = refs[:part_count]
    residual_ref, normed_ref, mix_ref, *out_refs = refs[-3 - part_count :]
    capacity, columns = out_refs[0].shape
    total = merged(part_refs[0][...])
    for part_ref in part_refs[1:]:
        total = total + merged(part_ref[...]).astype(jnp.float32)
    residual = total.astype(jnp.bfloat16)
    residual_ref[...] = residual.reshape(residual_ref.shape)
    res_float = residual.astype(jnp.float32)
    mean = jnp.mean(res_float * res_float, axis=-1, keepdims=True)
    normed = (res_float * lax.rsqrt(mean + 1e-05) * gain_ref[...]).astype(jnp.bfloat16)
    route = route_ref[...]
    normed_ref[:, :, :columns] = normed.reshape(residual_ref.shape)
    normed_ref[:, :, columns:] = route.reshape(normed_ref.shape[:2] + route.shape[1:])
    pick_and_mix(
        part_count,
        capacity,
        ctx_ref,
        plane_ref,
        normed,
        route.astype(jnp.float32),
        out_refs,
        mix_ref,
    )


def pick_shapes(ctx_count, capacity, tokens, columns):
    slot = jax.ShapeDtypeStruct((capacity, columns), jnp.bfloat16)
    return [jax.ShapeDtypeStruct((tokens, ctx_count * capacity), jnp.bfloat16)] + [slot] * ctx_count


def norm_and_pick(ctx_scalar, plane_scalars, gain, route, parts, capacity, after):
    _, half, columns = parts[0].shape
    tokens, extra = route.shape
    return pl.pallas_call(
        functools.partial(norm_kernel, len(parts)),
        out_shape=[
            jax.ShapeDtypeStruct((2, half, columns), jnp.bfloat16),
            jax.ShapeDtypeStruct((2, half, columns + extra), jnp.bfloat16),
        ]
        + pick_shapes(len(parts), capacity, tokens, columns),
        in_specs=[SMEM_SPEC] * 2 + [VMEM_SPEC] * (2 + len(parts)) + [ANY_SPEC] * len(after),
        out_specs=[VMEM_SPEC] * (3 + len(parts)),
        compiler_params=pltpu.CompilerParams(vmem_limit_bytes=12 << 20),
        cost_estimate=SMALL_COST,
    )(ctx_scalar, plane_scalars, gain, route, *parts, *after)


def pick_kernel(ctx_count, ctx_ref, plane_ref, held_ref, *refs):
    mix_ref, *out_refs = refs[-1 - ctx_count :]
    capacity, columns = out_refs[0].shape
    held = merged(held_ref[:, :, :columns])
    route = merged(held_ref[:, :, columns:]).astype(jnp.float32)
    pick_and_mix(ctx_count, capacity, ctx_ref, plane_ref, held, route, out_refs, mix_ref)


def pick_rows(ctx_scalar, plane_scalars, held, like, after):
    ctx_count = len(like)
    capacity, columns = like[0].shape
    return pl.pallas_call(
        functools.partial(pick_kernel, ctx_count),
        out_shape=pick_shapes(ctx_count, capacity, 2 * held.shape[1], columns),
        in_specs=[SMEM_SPEC] * 2 + [VMEM_SPEC] + [ANY_SPEC] * len(after),
        out_specs=[VMEM_SPEC] * (1 + ctx_count),
        compiler_params=pltpu.CompilerParams(vmem_limit_bytes=6 << 20),
        cost_estimate=SMALL_COST,
    )(ctx_scalar, plane_scalars, held, *after)


def expert_kernel(ctx_count, *refs):
    row_refs = refs[:ctx_count]
    gate_up_refs, down_refs = refs[ctx_count : ctx_count + 2], refs[ctx_count + 2 : ctx_count + 4]
    out_refs, activated_ref, total_ref = refs[-ctx_count - 2 : -2], refs[-2], refs[-1]
    capacity = row_refs[0].shape[0]
    routed = jnp.concatenate([row_ref[...] for row_ref in row_refs], axis=0)
    for side, gate_up_ref in enumerate(gate_up_refs):
        gate = nt_dot(routed, gate_up_ref[0])
        up = nt_dot(routed, gate_up_ref[1])
        activated = gate * jax.nn.sigmoid(1.702 * gate) * (up + 1.0)
        activated_ref[side] = activated.astype(jnp.bfloat16)
    total_ref[...] = nn_dot(activated_ref[0], down_refs[0][...])
    total = total_ref[...] + nn_dot(activated_ref[1], down_refs[1][...])
    for d, out_ref in enumerate(out_refs):
        out_ref[...] = total[d * capacity : (d + 1) * capacity].astype(jnp.bfloat16)


def expert(rows, gate_ups, downs, after):
    ctx_count = len(rows)
    capacity, columns = rows[0].shape
    half = downs[0].shape[0]
    count = ctx_count * capacity
    return pl.pallas_call(
        functools.partial(expert_kernel, ctx_count),
        out_shape=[jax.ShapeDtypeStruct((capacity, columns), jnp.bfloat16)] * ctx_count,
        in_specs=[VMEM_SPEC] * (ctx_count + 4) + [ANY_SPEC] * len(after),
        out_specs=[VMEM_SPEC] * ctx_count,
        scratch_shapes=[
            pltpu.VMEM((2, count, half), jnp.bfloat16),
            pltpu.VMEM((count, columns), jnp.float32),
        ],
        compiler_params=pltpu.CompilerParams(vmem_limit_bytes=16 << 20),
        cost_estimate=SMALL_COST,
    )(*rows, *gate_ups, *downs, *after)


def mix_kernel(ctx_count, extra_count, mix_ref, *refs):
    back_refs, extra_refs = refs[:ctx_count], refs[ctx_count : ctx_count + extra_count]
    out_ref = refs[-1]
    back = jnp.concatenate([back_ref[...] for back_ref in back_refs], axis=0)
    total = nn_dot(mix_ref[...], back)
    for extra_ref in extra_refs:
        total = total + merged(extra_ref[...]).astype(jnp.float32)
    out_ref[...] = total.astype(out_ref.dtype).reshape(out_ref.shape)


def mix_rows(mix, back, extra, after, dtype=jnp.bfloat16):
    tokens, count = mix.shape
    columns = back[0].shape[1]
    shape = (2, tokens // 2, columns)
    return pl.pallas_call(
        functools.partial(mix_kernel, len(back), len(extra)),
        out_shape=jax.ShapeDtypeStruct(shape, dtype),
        in_specs=[VMEM_SPEC] * (1 + len(back) + len(extra)) + [ANY_SPEC] * len(after),
        out_specs=VMEM_SPEC,
        compiler_params=pltpu.CompilerParams(vmem_limit_bytes=8 << 20),
        cost_estimate=SMALL_COST,
    )(mix, *back, *extra, *after)


def sum_kernel(part_count, *refs):
    total = refs[0][...]
    for part_ref in refs[1:part_count]:
        total = total + part_ref[...].astype(jnp.float32)
    refs[-1][...] = total.astype(jnp.bfloat16)


def sum_parts(parts, after):
    return pl.pallas_call(
        functools.partial(sum_kernel, len(parts)),
        out_shape=jax.ShapeDtypeStruct(parts[0].shape, jnp.bfloat16),
        in_specs=[VMEM_SPEC] * len(parts) + [ANY_SPEC] * len(after),
        out_specs=VMEM_SPEC,
        compiler_params=pltpu.CompilerParams(vmem_limit_bytes=4 << 20),
        cost_estimate=SMALL_COST,
    )(*parts, *after)


def local(
    queries,
    key_rows,
    value_matrix,
    hidden,
    out_weight,
    norm_gain,
    block_order,
    expert_ids,
    route_weights,
    gate_up_weight,
    down_weight,
):
    ctx_count = lax.axis_size("ctx")
    planes = lax.axis_size("exp") // 2
    ctx_scalar = lax.axis_index("ctx").astype(jnp.int32).reshape(1)
    plane_index = (lax.axis_index("exp") // 2).astype(jnp.int32)
    plane_scalars = jnp.stack([plane_index, jnp.full_like(plane_index, planes)])
    token_count = queries.shape[1]
    experts = ctx_count * planes
    capacity = 2 * token_count * TOPK // experts
    last = ctx_count - 1

    packed = pack(ctx_scalar, queries[0], key_rows[0], value_matrix[0], ctx_count)
    got = [ctx_swap(packed[d], d) for d in range(ctx_count)]
    weight = copy_after(jnp.swapaxes(out_weight, 0, 1), packed[:1])

    gate_up_mine = jnp.swapaxes(gate_up_weight[0], 0, 1)
    down_mine = down_weight[0]
    half = down_mine.shape[0]
    got, gate_up_mine, down_mine = lax.optimization_barrier((got, gate_up_mine, down_mine))

    partners = tuple(range(last, 0, -1))
    parts = list(attend(partners, ctx_scalar, block_order, weight, got, None, []))
    swapped = [core_swap(gate_up_mine), core_swap(down_mine)]
    hidden_columns = jnp.swapaxes(hidden[0], 0, 1)
    own = attend((0,), ctx_scalar, block_order, weight, got, hidden_columns, parts[:1])
    parts = [ctx_swap(part, last - i) for i, part in enumerate(parts)]
    other = [copy_after(w, list(own)) for w in swapped]
    gate_ups = [w.reshape(2, half, D) for w in (gate_up_mine, other[0])]
    downs = [down_mine, other[1]]

    route = jnp.concatenate(
        [expert_ids[0].astype(jnp.bfloat16), route_weights[0].astype(jnp.bfloat16)], axis=1
    )
    route = jnp.pad(route, ((0, 0), (0, -D % 128 - 2 * TOPK)))
    residual, held, mix, *rows = norm_and_pick(
        ctx_scalar, plane_scalars, norm_gain[None], route, list(own) + parts, capacity, other
    )

    def spread(blocks):
        return [ctx_swap(blocks[d], d) for d in range(ctx_count)]

    mixes = [mix]
    arrived = [spread(rows)]
    back = [None] * planes

    def run_expert(s, after):
        result = expert(arrived[s], gate_ups, downs, after)
        back[s] = spread(result)
        return list(result[:1])

    def run_mix(s, carried, after):
        part = mix_rows(mixes[s], back[s], carried, after)
        return [part], [plane_shift(part, 1)]

    done, carried = [], []
    for s in range(1, planes):
        held = plane_shift(held, 1)
        mix, *rows = pick_rows(ctx_scalar, plane_scalars, held, rows, arrived[s - 1][1:] + done)
        held, rows = lax.optimization_barrier((held, rows))
        mixes.append(mix)
        arrived.append(spread(rows))
        done = run_expert(s - 1, list(rows[:1]))
        if s == planes - 1:
            own = mix_rows(mixes[0], back[0], [residual], done, jnp.float32)
            done = [own]
        if s > 2:
            done, carried = run_mix(s - 2, carried, done)
    done = run_expert(planes - 1, done)
    for s in range(max(planes - 2, 1), planes):
        done, carried = run_mix(s, carried, done)
    out = sum_parts([own] + carried, [])
    return out.reshape(1, token_count, D)


def solution(mesh):
    return jax.shard_map(
        local,
        mesh=mesh,
        in_specs=(
            P("exp", "ctx", None),
            P("exp", "ctx", None),
            P("exp", "ctx", None),
            P("exp", "ctx", None),
            P("ctx", None),
            P(),
            P(),
            P("exp", "ctx", None),
            P("exp", "ctx", None),
            P(("ctx", "exp"), None, None),
            P(("ctx", "exp"), None, None),
        ),
        out_specs=P("exp", "ctx", None),
        check_vma=False,
    )
```

```python
import functools

import jax
import jax.numpy as jnp
from jax import lax
from jax.experimental import pallas as pl
from jax.experimental.pallas import tpu as pltpu
from jax.sharding import PartitionSpec as P

D = 2880
QUERY_HEADS = 32
KEY_VALUE_HEADS = 4
HEAD_SIZE = 64
TOPK = 4


negative_large = -1e30


def ctx_swap(rows, distance):
    if distance == 0:
        return rows
    count = lax.axis_size("ctx")
    return lax.ppermute(rows, "ctx", [(i, i ^ distance) for i in range(count)])


def plane_shift(rows, planes):
    count = lax.axis_size("exp")
    if (2 * planes) % count == 0:
        return rows
    return lax.ppermute(rows, "exp", [(i, (i + 2 * planes) % count) for i in range(count)])


def core_swap(rows):
    count = lax.axis_size("exp")
    return lax.ppermute(rows, "exp", [(i, i ^ 1) for i in range(count)])

ANY_SPEC = pl.BlockSpec(memory_space=pl.ANY)
SMEM_SPEC = pl.BlockSpec(memory_space=pltpu.SMEM)
VMEM_SPEC = pl.BlockSpec(memory_space=pltpu.VMEM)
SMALL_COST = pl.CostEstimate(flops=1, bytes_accessed=1, transcendentals=0)


def nt_dot(left, right):
    return lax.dot_general(
        left, right, (((1,), (1,)), ((), ())), preferred_element_type=jnp.float32
    )


def nn_dot(left, right):
    return jnp.dot(left, right, preferred_element_type=jnp.float32)


def merged(block):
    return block.reshape(block.shape[0] * block.shape[1], block.shape[2])


def pack_kernel(ctx_count, ctx_ref, q_ref, k_ref, v_ref, *out_refs):
    heads_here = QUERY_HEADS // ctx_count
    group = QUERY_HEADS // KEY_VALUE_HEADS
    width = heads_here * HEAD_SIZE
    rows = q_ref.shape[0]
    low = lax.broadcasted_iota(jnp.int32, (rows, 2 * HEAD_SIZE), 1) < HEAD_SIZE
    for d in range(ctx_count):
        to = ctx_ref[0] ^ d
        head = (to * heads_here) // group
        odd = (head % 2) == 1
        pair = pl.ds(pl.multiple_of((head // 2) * 2 * HEAD_SIZE, 2 * HEAD_SIZE), 2 * HEAD_SIZE)
        keys = k_ref[:, pair].astype(jnp.float32)
        values = v_ref[:, pair].astype(jnp.float32)
        keys = jnp.where(odd, pltpu.roll(keys, HEAD_SIZE, 1), keys)
        values = jnp.where(odd, values, pltpu.roll(values, HEAD_SIZE, 1))
        columns = pl.ds(pl.multiple_of(to * width, width), width)
        out_refs[d][:, :width] = q_ref[:, columns]
        out_refs[d][:, width:] = jnp.where(low, keys, values).astype(jnp.bfloat16)


def pack(ctx_scalar, queries, keys, values, ctx_count):
    rows, width = queries.shape[0], queries.shape[1] // ctx_count
    shape = jax.ShapeDtypeStruct((rows, width + 2 * HEAD_SIZE), jnp.bfloat16)
    return pl.pallas_call(
        functools.partial(pack_kernel, ctx_count),
        out_shape=[shape] * ctx_count,
        in_specs=[SMEM_SPEC] + [VMEM_SPEC] * 3,
        out_specs=[VMEM_SPEC] * ctx_count,
        compiler_params=pltpu.CompilerParams(vmem_limit_bytes=4 << 20),
        cost_estimate=SMALL_COST,
    )(ctx_scalar, queries, keys, values)


def copy_kernel(source_ref, *refs):
    refs[-1][...] = source_ref[...]


def copy_after(source, after):
    return pl.pallas_call(
        copy_kernel,
        out_shape=jax.ShapeDtypeStruct(source.shape, source.dtype),
        in_specs=[VMEM_SPEC] + [ANY_SPEC] * len(after),
        out_specs=VMEM_SPEC,
        compiler_params=pltpu.CompilerParams(vmem_limit_bytes=20 << 20),
        cost_estimate=SMALL_COST,
    )(source, *after)


def attend_kernel(dests, ctx_count, ctx_ref, order_ref, weight_ref, *refs):
    got_refs, hidden_ref, out_refs = refs[:ctx_count], refs[ctx_count], refs[-len(dests) :]
    heads_here = QUERY_HEADS // ctx_count
    width = heads_here * HEAD_SIZE
    rows = got_refs[0].shape[0]
    block = rows // 2
    me = ctx_ref[0]
    lanes = lax.broadcasted_iota(jnp.int32, (rows, 2 * HEAD_SIZE), 1) < HEAD_SIZE
    keys, values, key_pos = [], [], []
    place = lax.broadcasted_iota(jnp.int32, (1, rows), 1)
    for d in range(ctx_count):
        both = got_refs[d][:, width:].astype(jnp.float32)
        other = pltpu.roll(both, HEAD_SIZE, 1)
        scaled = jnp.where(lanes, both, other) * HEAD_SIZE ** (-0.5)
        keys.append(scaled.astype(jnp.bfloat16))
        values.append(jnp.where(lanes, other, both).astype(jnp.bfloat16))
        slot = 2 * (me ^ d)
        first, second = order_ref[slot] * block, order_ref[slot + 1] * block - block
        key_pos.append(place + jnp.where(place < block, first, second))
    keys = jnp.concatenate(keys, axis=0)
    values = jnp.concatenate(values, axis=0)
    key_pos = jnp.concatenate(key_pos, axis=1)
    row = lax.broadcasted_iota(jnp.int32, (rows, 1), 0)
    for out_ref, d in zip(out_refs, dests):
        slot = 2 * (me ^ d)
        first, second = order_ref[slot] * block, order_ref[slot + 1] * block - block
        query_pos = row + jnp.where(row < block, first, second)
        visible = jnp.concatenate([key_pos <= query_pos] * heads_here, axis=0)
        stacked = []
        for pair in range(heads_here // 2):
            both = got_refs[d][:, pair * 2 * HEAD_SIZE : (pair + 1) * 2 * HEAD_SIZE]
            for side in range(2):
                stacked.append(jnp.where(lanes == (side == 0), both, jnp.zeros_like(both)))
        scores = nt_dot(jnp.concatenate(stacked, axis=0), keys)
        scores = jnp.where(visible, scores, negative_large)
        probs = jnp.exp(scores - jnp.max(scores, axis=-1, keepdims=True))
        total = jnp.sum(probs, axis=-1, keepdims=True)
        mixed = nn_dot(probs.astype(jnp.bfloat16), values) / total
        attended = []
        for pair in range(heads_here // 2):
            sides = [mixed[(2 * pair + i) * rows : (2 * pair + i + 1) * rows] for i in range(2)]
            attended.append(jnp.where(lanes, sides[0], sides[1]).astype(jnp.bfloat16))
        part = nt_dot(jnp.concatenate(attended, axis=1), weight_ref[...])
        if d == 0:
            eye = lax.broadcasted_iota(jnp.int32, (rows, rows), 1) == row
            part = part + nt_dot(eye.astype(jnp.bfloat16), hidden_ref[...])
        out_ref[...] = part.astype(out_ref.dtype).reshape(out_ref.shape)


def attend(dests, ctx_scalar, order, weight, got, hidden, after):
    ctx_count = len(got)
    rows, columns = got[0].shape[0], weight.shape[0]
    shapes = [
        jax.ShapeDtypeStruct((2, rows // 2, columns), jnp.bfloat16 if d else jnp.float32)
        for d in dests
    ]
    extra = [hidden] if 0 in dests else []
    work = len(dests) * rows * weight.shape[1]
    return pl.pallas_call(
        functools.partial(attend_kernel, dests, ctx_count),
        out_shape=shapes,
        in_specs=[SMEM_SPEC, SMEM_SPEC]
        + [VMEM_SPEC] * (1 + ctx_count + len(extra))
        + [ANY_SPEC] * len(after),
        out_specs=[VMEM_SPEC] * len(dests),
        compiler_params=pltpu.CompilerParams(vmem_limit_bytes=20 << 20),
        cost_estimate=SMALL_COST,
    )(ctx_scalar, order, weight, *got, *extra, *after)


def pick_and_mix(ctx_count, capacity, ctx_ref, plane_ref, held, route, out_refs, mix_ref):
    tokens = held.shape[0]
    count = ctx_count * capacity
    lane = lax.broadcasted_iota(jnp.int32, (1, count), 1)
    partner = ctx_ref[0] ^ (lane // capacity)
    wanted = (partner * plane_ref[1] + plane_ref[0]).astype(jnp.float32)
    member = jnp.zeros((tokens, count), jnp.float32)
    weight = jnp.zeros((tokens, count), jnp.float32)
    for k in range(TOPK):
        chosen = route[:, k : k + 1] == wanted
        member = jnp.where(chosen, 1.0, member)
        weight = jnp.where(chosen, route[:, TOPK + k : TOPK + k + 1], weight)
    row = lax.broadcasted_iota(jnp.int32, (tokens, tokens), 0)
    earlier = lax.broadcasted_iota(jnp.int32, (tokens, tokens), 1) < row
    rank = nn_dot(earlier.astype(jnp.bfloat16), member.astype(jnp.bfloat16))
    slot = (lane % capacity).astype(jnp.float32)
    placed = jnp.where(rank == slot, member, 0.0)
    mix_ref[...] = (placed * weight).astype(jnp.bfloat16)
    picked = nn_dot(placed.T.astype(jnp.bfloat16), held).astype(jnp.bfloat16)
    for d, out_ref in enumerate(out_refs):
        out_ref[...] = picked[d * capacity : (d + 1) * capacity]


def norm_kernel(part_count, ctx_ref, plane_ref, gain_ref, route_ref, *refs):
    part_refs = refs[:part_count]
    residual_ref, normed_ref, mix_ref, *out_refs = refs[-3 - part_count :]
    capacity, columns = out_refs[0].shape
    total = merged(part_refs[0][...])
    for part_ref in part_refs[1:]:
        total = total + merged(part_ref[...]).astype(jnp.float32)
    residual = total.astype(jnp.bfloat16)
    residual_ref[...] = residual.reshape(residual_ref.shape)
    res_float = residual.astype(jnp.float32)
    mean = jnp.mean(res_float * res_float, axis=-1, keepdims=True)
    normed = (res_float * lax.rsqrt(mean + 1e-05) * gain_ref[...]).astype(jnp.bfloat16)
    route = route_ref[...]
    normed_ref[:, :, :columns] = normed.reshape(residual_ref.shape)
    normed_ref[:, :, columns:] = route.reshape(normed_ref.shape[:2] + route.shape[1:])
    pick_and_mix(
        part_count,
        capacity,
        ctx_ref,
        plane_ref,
        normed,
        route.astype(jnp.float32),
        out_refs,
        mix_ref,
    )


def pick_shapes(ctx_count, capacity, tokens, columns):
    slot = jax.ShapeDtypeStruct((capacity, columns), jnp.bfloat16)
    return [jax.ShapeDtypeStruct((tokens, ctx_count * capacity), jnp.bfloat16)] + [slot] * ctx_count


def norm_and_pick(ctx_scalar, plane_scalars, gain, route, parts, capacity, after):
    _, half, columns = parts[0].shape
    tokens, extra = route.shape
    return pl.pallas_call(
        functools.partial(norm_kernel, len(parts)),
        out_shape=[
            jax.ShapeDtypeStruct((2, half, columns), jnp.bfloat16),
            jax.ShapeDtypeStruct((2, half, columns + extra), jnp.bfloat16),
        ]
        + pick_shapes(len(parts), capacity, tokens, columns),
        in_specs=[SMEM_SPEC] * 2 + [VMEM_SPEC] * (2 + len(parts)) + [ANY_SPEC] * len(after),
        out_specs=[VMEM_SPEC] * (3 + len(parts)),
        compiler_params=pltpu.CompilerParams(vmem_limit_bytes=12 << 20),
        cost_estimate=SMALL_COST,
    )(ctx_scalar, plane_scalars, gain, route, *parts, *after)


def pick_kernel(ctx_count, ctx_ref, plane_ref, held_ref, *refs):
    mix_ref, *out_refs = refs[-1 - ctx_count :]
    capacity, columns = out_refs[0].shape
    held = merged(held_ref[:, :, :columns])
    route = merged(held_ref[:, :, columns:]).astype(jnp.float32)
    pick_and_mix(ctx_count, capacity, ctx_ref, plane_ref, held, route, out_refs, mix_ref)


def pick_rows(ctx_scalar, plane_scalars, held, like, after):
    ctx_count = len(like)
    capacity, columns = like[0].shape
    return pl.pallas_call(
        functools.partial(pick_kernel, ctx_count),
        out_shape=pick_shapes(ctx_count, capacity, 2 * held.shape[1], columns),
        in_specs=[SMEM_SPEC] * 2 + [VMEM_SPEC] + [ANY_SPEC] * len(after),
        out_specs=[VMEM_SPEC] * (1 + ctx_count),
        compiler_params=pltpu.CompilerParams(vmem_limit_bytes=6 << 20),
        cost_estimate=SMALL_COST,
    )(ctx_scalar, plane_scalars, held, *after)


def expert_kernel(ctx_count, *refs):
    row_refs = refs[:ctx_count]
    gate_up_refs, down_refs = refs[ctx_count : ctx_count + 2], refs[ctx_count + 2 : ctx_count + 4]
    out_refs, activated_ref, total_ref = refs[-ctx_count - 2 : -2], refs[-2], refs[-1]
    capacity = row_refs[0].shape[0]
    routed = jnp.concatenate([row_ref[...] for row_ref in row_refs], axis=0)
    for side, gate_up_ref in enumerate(gate_up_refs):
        gate = nt_dot(routed, gate_up_ref[0])
        up = nt_dot(routed, gate_up_ref[1])
        activated = gate * jax.nn.sigmoid(1.702 * gate) * (up + 1.0)
        activated_ref[side] = activated.astype(jnp.bfloat16)
    total_ref[...] = nn_dot(activated_ref[0], down_refs[0][...])
    total = total_ref[...] + nn_dot(activated_ref[1], down_refs[1][...])
    for d, out_ref in enumerate(out_refs):
        out_ref[...] = total[d * capacity : (d + 1) * capacity].astype(jnp.bfloat16)


def expert(rows, gate_ups, downs, after):
    ctx_count = len(rows)
    capacity, columns = rows[0].shape
    half = downs[0].shape[0]
    count = ctx_count * capacity
    return pl.pallas_call(
        functools.partial(expert_kernel, ctx_count),
        out_shape=[jax.ShapeDtypeStruct((capacity, columns), jnp.bfloat16)] * ctx_count,
        in_specs=[VMEM_SPEC] * (ctx_count + 4) + [ANY_SPEC] * len(after),
        out_specs=[VMEM_SPEC] * ctx_count,
        scratch_shapes=[
            pltpu.VMEM((2, count, half), jnp.bfloat16),
            pltpu.VMEM((count, columns), jnp.float32),
        ],
        compiler_params=pltpu.CompilerParams(vmem_limit_bytes=16 << 20),
        cost_estimate=SMALL_COST,
    )(*rows, *gate_ups, *downs, *after)


def mix_kernel(ctx_count, extra_count, mix_ref, *refs):
    back_refs, extra_refs = refs[:ctx_count], refs[ctx_count : ctx_count + extra_count]
    out_ref = refs[-1]
    back = jnp.concatenate([back_ref[...] for back_ref in back_refs], axis=0)
    total = nn_dot(mix_ref[...], back)
    for extra_ref in extra_refs:
        total = total + merged(extra_ref[...]).astype(jnp.float32)
    out_ref[...] = total.astype(out_ref.dtype).reshape(out_ref.shape)


def mix_rows(mix, back, extra, after, dtype=jnp.bfloat16):
    tokens, count = mix.shape
    columns = back[0].shape[1]
    shape = (2, tokens // 2, columns)
    return pl.pallas_call(
        functools.partial(mix_kernel, len(back), len(extra)),
        out_shape=jax.ShapeDtypeStruct(shape, dtype),
        in_specs=[VMEM_SPEC] * (1 + len(back) + len(extra)) + [ANY_SPEC] * len(after),
        out_specs=VMEM_SPEC,
        compiler_params=pltpu.CompilerParams(vmem_limit_bytes=8 << 20),
        cost_estimate=SMALL_COST,
    )(mix, *back, *extra, *after)


def sum_kernel(part_count, *refs):
    total = refs[0][...]
    for part_ref in refs[1:part_count]:
        total = total + part_ref[...].astype(jnp.float32)
    refs[-1][...] = total.astype(jnp.bfloat16)


def sum_parts(parts, after):
    return pl.pallas_call(
        functools.partial(sum_kernel, len(parts)),
        out_shape=jax.ShapeDtypeStruct(parts[0].shape, jnp.bfloat16),
        in_specs=[VMEM_SPEC] * len(parts) + [ANY_SPEC] * len(after),
        out_specs=VMEM_SPEC,
        compiler_params=pltpu.CompilerParams(vmem_limit_bytes=4 << 20),
        cost_estimate=SMALL_COST,
    )(*parts, *after)


def local(
    queries,
    key_rows,
    value_matrix,
    hidden,
    out_weight,
    norm_gain,
    block_order,
    expert_ids,
    route_weights,
    gate_up_weight,
    down_weight,
):
    ctx_count = lax.axis_size("ctx")
    planes = lax.axis_size("exp") // 2
    ctx_scalar = lax.axis_index("ctx").astype(jnp.int32).reshape(1)
    plane_index = (lax.axis_index("exp") // 2).astype(jnp.int32)
    plane_scalars = jnp.stack([plane_index, jnp.full_like(plane_index, planes)])
    token_count = queries.shape[1]
    experts = ctx_count * planes
    capacity = 2 * token_count * TOPK // experts
    last = ctx_count - 1

    packed = pack(ctx_scalar, queries[0], key_rows[0], value_matrix[0], ctx_count)
    got = [ctx_swap(packed[d], d) for d in range(ctx_count)]
    weight = copy_after(jnp.swapaxes(out_weight, 0, 1), packed[:1])

    gate_up_mine = jnp.swapaxes(gate_up_weight[0], 0, 1)
    down_mine = down_weight[0]
    half = down_mine.shape[0]
    got, gate_up_mine, down_mine = lax.optimization_barrier((got, gate_up_mine, down_mine))

    partners = tuple(range(last, 0, -1))
    parts = list(attend(partners, ctx_scalar, block_order, weight, got, None, []))
    swapped = [core_swap(gate_up_mine), core_swap(down_mine)]
    hidden_columns = jnp.swapaxes(hidden[0], 0, 1)
    own = attend((0,), ctx_scalar, block_order, weight, got, hidden_columns, parts[:1])
    parts = [ctx_swap(part, last - i) for i, part in enumerate(parts)]
    other = [copy_after(w, list(own)) for w in swapped]
    gate_ups = [w.reshape(2, half, D) for w in (gate_up_mine, other[0])]
    downs = [down_mine, other[1]]

    route = jnp.concatenate(
        [expert_ids[0].astype(jnp.bfloat16), route_weights[0].astype(jnp.bfloat16)], axis=1
    )
    route = jnp.pad(route, ((0, 0), (0, -D % 128 - 2 * TOPK)))
    residual, held, mix, *rows = norm_and_pick(
        ctx_scalar, plane_scalars, norm_gain[None], route, list(own) + parts, capacity, other
    )

    def spread(blocks):
        return [ctx_swap(blocks[d], d) for d in range(ctx_count)]

    mixes = [mix]
    arrived = [spread(rows)]
    back = [None] * planes

    def run_expert(s, after):
        result = expert(arrived[s], gate_ups, downs, after)
        if s > 0:
            back[s] = spread(result)
        return list(result)

    def run_mix(s, carried, after):
        part = mix_rows(mixes[s], back[s], carried, after)
        return [part], [plane_shift(part, 1)]

    done, carried = [], []
    for s in range(1, planes):
        held = plane_shift(held, 1)
        mix, *rows = pick_rows(ctx_scalar, plane_scalars, held, rows, arrived[s - 1][1:] + done[:1])
        held, rows = lax.optimization_barrier((held, rows))
        mixes.append(mix)
        arrived.append(spread(rows))
        done = run_expert(s - 1, list(rows[:1]))
        if s == 1:
            own_result = done
        if s > 2:
            done, carried = run_mix(s - 2, carried, done)
    done = run_expert(planes - 1, done)
    own_result, _ = lax.optimization_barrier((own_result, done))
    back[0] = spread(own_result)
    for s in range(max(planes - 2, 1), planes):
        done, carried = run_mix(s, carried, done)
    own = mix_rows(mixes[0], back[0], [residual], done, jnp.float32)
    out = sum_parts([own] + carried, [])
    return out.reshape(1, token_count, D)


def solution(mesh):
    return jax.shard_map(
        local,
        mesh=mesh,
        in_specs=(
            P("exp", "ctx", None),
            P("exp", "ctx", None),
            P("exp", "ctx", None),
            P("exp", "ctx", None),
            P("ctx", None),
            P(),
            P(),
            P("exp", "ctx", None),
            P("exp", "ctx", None),
            P(("ctx", "exp"), None, None),
            P(("ctx", "exp"), None, None),
        ),
        out_specs=P("exp", "ctx", None),
        check_vma=False,
    )
```

```python
import functools

import jax
import jax.numpy as jnp
from jax import lax
from jax.experimental import pallas as pl
from jax.experimental.pallas import tpu as pltpu
from jax.sharding import PartitionSpec as P

D = 2880
QUERY_HEADS = 32
KEY_VALUE_HEADS = 4
HEAD_SIZE = 64
TOPK = 4


negative_large = -1e30


def ctx_swap(rows, distance):
    if distance == 0:
        return rows
    count = lax.axis_size("ctx")
    return lax.ppermute(rows, "ctx", [(i, i ^ distance) for i in range(count)])


def plane_shift(rows, planes):
    count = lax.axis_size("exp")
    if (2 * planes) % count == 0:
        return rows
    return lax.ppermute(rows, "exp", [(i, (i + 2 * planes) % count) for i in range(count)])


def core_swap(rows):
    count = lax.axis_size("exp")
    return lax.ppermute(rows, "exp", [(i, i ^ 1) for i in range(count)])

ANY_SPEC = pl.BlockSpec(memory_space=pl.ANY)
SMEM_SPEC = pl.BlockSpec(memory_space=pltpu.SMEM)
VMEM_SPEC = pl.BlockSpec(memory_space=pltpu.VMEM)
SMALL_COST = pl.CostEstimate(flops=1, bytes_accessed=1, transcendentals=0)


def nt_dot(left, right):
    return lax.dot_general(
        left, right, (((1,), (1,)), ((), ())), preferred_element_type=jnp.float32
    )


def nn_dot(left, right):
    return jnp.dot(left, right, preferred_element_type=jnp.float32)


def merged(block):
    return block.reshape(block.shape[0] * block.shape[1], block.shape[2])


def start_copies(pairs, sems, first=0):
    copies = [
        pltpu.make_async_copy(source, target, sems.at[first + i])
        for i, (source, target) in enumerate(pairs)
    ]
    for copy in copies:
        copy.start()
    return copies


def pack_kernel(ctx_count, ctx_ref, q_ref, k_ref, v_ref, *refs):
    out_refs, (q_buf, k_buf, v_buf, sems) = refs[:ctx_count], refs[ctx_count:]
    heads_here = QUERY_HEADS // ctx_count
    group = QUERY_HEADS // KEY_VALUE_HEADS
    width = heads_here * HEAD_SIZE
    rows = q_ref.shape[0]
    for copy in start_copies([(k_ref, k_buf), (v_ref, v_buf), (q_ref, q_buf)], sems):
        copy.wait()
    low = lax.broadcasted_iota(jnp.int32, (rows, 2 * HEAD_SIZE), 1) < HEAD_SIZE
    for d in range(ctx_count):
        to = ctx_ref[0] ^ d
        head = (to * heads_here) // group
        odd = (head % 2) == 1
        pair = pl.ds(pl.multiple_of((head // 2) * 2 * HEAD_SIZE, 2 * HEAD_SIZE), 2 * HEAD_SIZE)
        keys = k_buf[:, pair].astype(jnp.float32)
        values = v_buf[:, pair].astype(jnp.float32)
        keys = jnp.where(odd, pltpu.roll(keys, HEAD_SIZE, 1), keys)
        values = jnp.where(odd, values, pltpu.roll(values, HEAD_SIZE, 1))
        columns = pl.ds(pl.multiple_of(to * width, width), width)
        out_refs[d][:, :width] = q_buf[:, columns]
        out_refs[d][:, width:] = jnp.where(low, keys, values).astype(jnp.bfloat16)


def pack(ctx_scalar, queries, keys, values, ctx_count):
    rows, width = queries.shape[0], queries.shape[1] // ctx_count
    shape = jax.ShapeDtypeStruct((rows, width + 2 * HEAD_SIZE), jnp.bfloat16)
    return pl.pallas_call(
        functools.partial(pack_kernel, ctx_count),
        out_shape=[shape] * ctx_count,
        in_specs=[SMEM_SPEC] + [ANY_SPEC] * 3,
        out_specs=[VMEM_SPEC] * ctx_count,
        scratch_shapes=[pltpu.VMEM(x.shape, x.dtype) for x in (queries, keys, values)]
        + [pltpu.SemaphoreType.DMA((3,))],
        compiler_params=pltpu.CompilerParams(vmem_limit_bytes=56 << 20),
        cost_estimate=SMALL_COST,
    )(ctx_scalar, queries, keys, values)


def copy_kernel(source_ref, *refs):
    refs[-1][...] = source_ref[...]


def copy_after(source, after):
    return pl.pallas_call(
        copy_kernel,
        out_shape=jax.ShapeDtypeStruct(source.shape, source.dtype),
        in_specs=[VMEM_SPEC] + [ANY_SPEC] * len(after),
        out_specs=VMEM_SPEC,
        compiler_params=pltpu.CompilerParams(vmem_limit_bytes=20 << 20),
        cost_estimate=SMALL_COST,
    )(source, *after)


def attend_kernel(dests, ctx_count, ctx_ref, order_ref, weight_ref, *refs):
    out_refs, (weight_buf, got_refs, sems) = refs[-3 - len(dests) : -3], refs[-3:]
    hidden_ref = refs[ctx_count]
    copies = start_copies([(refs[d], got_refs.at[d]) for d in range(ctx_count)], sems)
    weight_copy = start_copies([(weight_ref, weight_buf)], sems, ctx_count)[0]
    for copy in copies:
        copy.wait()
    heads_here = QUERY_HEADS // ctx_count
    width = heads_here * HEAD_SIZE
    rows = got_refs.shape[1]
    block = rows // 2
    me = ctx_ref[0]
    lanes = lax.broadcasted_iota(jnp.int32, (rows, 2 * HEAD_SIZE), 1) < HEAD_SIZE
    keys, values, key_pos = [], [], []
    place = lax.broadcasted_iota(jnp.int32, (1, rows), 1)
    for d in range(ctx_count):
        both = got_refs[d, :, width:].astype(jnp.float32)
        other = pltpu.roll(both, HEAD_SIZE, 1)
        scaled = jnp.where(lanes, both, other) * HEAD_SIZE ** (-0.5)
        keys.append(scaled.astype(jnp.bfloat16))
        values.append(jnp.where(lanes, other, both).astype(jnp.bfloat16))
        slot = 2 * (me ^ d)
        first, second = order_ref[slot] * block, order_ref[slot + 1] * block - block
        key_pos.append(place + jnp.where(place < block, first, second))
    keys = jnp.concatenate(keys, axis=0)
    values = jnp.concatenate(values, axis=0)
    key_pos = jnp.concatenate(key_pos, axis=1)
    row = lax.broadcasted_iota(jnp.int32, (rows, 1), 0)
    stacked, visible, attended = [], [], []
    for d in dests:
        slot = 2 * (me ^ d)
        first, second = order_ref[slot] * block, order_ref[slot + 1] * block - block
        query_pos = row + jnp.where(row < block, first, second)
        visible += [key_pos <= query_pos] * heads_here
        for pair in range(heads_here // 2):
            both = got_refs[d, :, pair * 2 * HEAD_SIZE : (pair + 1) * 2 * HEAD_SIZE]
            for side in range(2):
                stacked.append(jnp.where(lanes == (side == 0), both, jnp.zeros_like(both)))
    scores = nt_dot(jnp.concatenate(stacked, axis=0), keys)
    scores = jnp.where(jnp.concatenate(visible, axis=0), scores, negative_large)
    probs = jnp.exp(scores - jnp.max(scores, axis=-1, keepdims=True))
    total = jnp.sum(probs, axis=-1, keepdims=True)
    mixed = nn_dot(probs.astype(jnp.bfloat16), values) / total
    mixed = [mixed[i * rows : (i + 1) * rows] for i in range(len(stacked))]
    for i in range(len(dests)):
        pairs = []
        for head in range(i * heads_here, (i + 1) * heads_here, 2):
            pairs.append(jnp.where(lanes, mixed[head], mixed[head + 1]).astype(jnp.bfloat16))
        attended.append(jnp.concatenate(pairs, axis=1))
    weight_copy.wait()
    parts = nt_dot(jnp.concatenate(attended, axis=0), weight_buf[...])
    for i, (out_ref, d) in enumerate(zip(out_refs, dests)):
        part = parts[i * rows : (i + 1) * rows]
        if d == 0:
            eye = lax.broadcasted_iota(jnp.int32, (rows, rows), 1) == row
            part = part + nt_dot(eye.astype(jnp.bfloat16), hidden_ref[...])
        out_ref[...] = part.astype(out_ref.dtype).reshape(out_ref.shape)


def attend(dests, ctx_scalar, order, weight, got, hidden, after):
    ctx_count = len(got)
    rows, columns = got[0].shape[0], weight.shape[0]
    shapes = [
        jax.ShapeDtypeStruct((2, rows // 2, columns), jnp.bfloat16 if d else jnp.float32)
        for d in dests
    ]
    extra = [hidden] if 0 in dests else []
    work = len(dests) * rows * weight.shape[1]
    return pl.pallas_call(
        functools.partial(attend_kernel, dests, ctx_count),
        out_shape=shapes,
        in_specs=[SMEM_SPEC, SMEM_SPEC]
        + [ANY_SPEC] * (1 + ctx_count)
        + [VMEM_SPEC] * len(extra)
        + [ANY_SPEC] * len(after),
        out_specs=[VMEM_SPEC] * len(dests),
        scratch_shapes=[
            pltpu.VMEM(weight.shape, weight.dtype),
            pltpu.VMEM((ctx_count,) + got[0].shape, got[0].dtype),
            pltpu.SemaphoreType.DMA((ctx_count + 1,)),
        ],
        compiler_params=pltpu.CompilerParams(vmem_limit_bytes=56 << 20),
        cost_estimate=SMALL_COST,
    )(ctx_scalar, order, weight, *got, *extra, *after)


def pick_and_mix(ctx_count, capacity, ctx_ref, plane_ref, held, route, out_refs, mix_ref):
    tokens = held.shape[0]
    count = ctx_count * capacity
    lane = lax.broadcasted_iota(jnp.int32, (1, count), 1)
    partner = ctx_ref[0] ^ (lane // capacity)
    wanted = (partner * plane_ref[1] + plane_ref[0]).astype(jnp.float32)
    member = jnp.zeros((tokens, count), jnp.float32)
    weight = jnp.zeros((tokens, count), jnp.float32)
    for k in range(TOPK):
        chosen = route[:, k : k + 1] == wanted
        member = jnp.where(chosen, 1.0, member)
        weight = jnp.where(chosen, route[:, TOPK + k : TOPK + k + 1], weight)
    row = lax.broadcasted_iota(jnp.int32, (tokens, tokens), 0)
    earlier = lax.broadcasted_iota(jnp.int32, (tokens, tokens), 1) < row
    rank = nn_dot(earlier.astype(jnp.bfloat16), member.astype(jnp.bfloat16))
    slot = (lane % capacity).astype(jnp.float32)
    placed = jnp.where(rank == slot, member, 0.0)
    mix_ref[...] = (placed * weight).astype(jnp.bfloat16)
    picked = nn_dot(placed.T.astype(jnp.bfloat16), held).astype(jnp.bfloat16)
    for d, out_ref in enumerate(out_refs):
        out_ref[...] = picked[d * capacity : (d + 1) * capacity]


def norm_kernel(part_count, ctx_ref, plane_ref, gain_ref, route_ref, *refs):
    part_refs = refs[:part_count]
    residual_ref, normed_ref, mix_ref, *out_refs = refs[-3 - part_count :]
    capacity, columns = out_refs[0].shape
    total = merged(part_refs[0][...])
    for part_ref in part_refs[1:]:
        total = total + merged(part_ref[...]).astype(jnp.float32)
    residual = total.astype(jnp.bfloat16)
    residual_ref[...] = residual.reshape(residual_ref.shape)
    res_float = residual.astype(jnp.float32)
    mean = jnp.mean(res_float * res_float, axis=-1, keepdims=True)
    normed = (res_float * lax.rsqrt(mean + 1e-05) * gain_ref[...]).astype(jnp.bfloat16)
    route = route_ref[...]
    normed_ref[:, :, :columns] = normed.reshape(residual_ref.shape)
    normed_ref[:, :, columns:] = route.reshape(normed_ref.shape[:2] + route.shape[1:])
    pick_and_mix(
        part_count,
        capacity,
        ctx_ref,
        plane_ref,
        normed,
        route.astype(jnp.float32),
        out_refs,
        mix_ref,
    )


def pick_shapes(ctx_count, capacity, tokens, columns):
    slot = jax.ShapeDtypeStruct((capacity, columns), jnp.bfloat16)
    return [jax.ShapeDtypeStruct((tokens, ctx_count * capacity), jnp.bfloat16)] + [slot] * ctx_count


def norm_and_pick(ctx_scalar, plane_scalars, gain, route, parts, capacity, after):
    _, half, columns = parts[0].shape
    tokens, extra = route.shape
    return pl.pallas_call(
        functools.partial(norm_kernel, len(parts)),
        out_shape=[
            jax.ShapeDtypeStruct((2, half, columns), jnp.bfloat16),
            jax.ShapeDtypeStruct((2, half, columns + extra), jnp.bfloat16),
        ]
        + pick_shapes(len(parts), capacity, tokens, columns),
        in_specs=[SMEM_SPEC] * 2 + [VMEM_SPEC] * (2 + len(parts)) + [ANY_SPEC] * len(after),
        out_specs=[VMEM_SPEC] * (3 + len(parts)),
        compiler_params=pltpu.CompilerParams(vmem_limit_bytes=12 << 20),
        cost_estimate=SMALL_COST,
    )(ctx_scalar, plane_scalars, gain, route, *parts, *after)


def pick_kernel(ctx_count, ctx_ref, plane_ref, held_ref, *refs):
    mix_ref, *out_refs = refs[-1 - ctx_count :]
    capacity, columns = out_refs[0].shape
    held = merged(held_ref[:, :, :columns])
    route = merged(held_ref[:, :, columns:]).astype(jnp.float32)
    pick_and_mix(ctx_count, capacity, ctx_ref, plane_ref, held, route, out_refs, mix_ref)


def pick_rows(ctx_scalar, plane_scalars, held, like, after):
    ctx_count = len(like)
    capacity, columns = like[0].shape
    return pl.pallas_call(
        functools.partial(pick_kernel, ctx_count),
        out_shape=pick_shapes(ctx_count, capacity, 2 * held.shape[1], columns),
        in_specs=[SMEM_SPEC] * 2 + [VMEM_SPEC] + [ANY_SPEC] * len(after),
        out_specs=[VMEM_SPEC] * (1 + ctx_count),
        compiler_params=pltpu.CompilerParams(vmem_limit_bytes=6 << 20),
        cost_estimate=SMALL_COST,
    )(ctx_scalar, plane_scalars, held, *after)


def expert_kernel(ctx_count, tile, *refs):
    row_refs, refs = refs[:ctx_count], refs[ctx_count:]
    gate_up_refs, down_refs = refs[:2], refs[2:4]
    out_refs, total_ref = refs[-ctx_count - 1 : -1], refs[-1]
    capacity = row_refs[0].shape[0]

    def add_tile(i, carry):
        routed = jnp.concatenate([row_ref[...] for row_ref in row_refs], axis=0)
        here = pl.ds(pl.multiple_of(i * tile, tile), tile)
        added = None
        for gate_up_ref, down_ref in zip(gate_up_refs, down_refs):
            gate = nt_dot(routed, gate_up_ref[0, here])
            up = nt_dot(routed, gate_up_ref[1, here])
            activated = gate * jax.nn.sigmoid(1.702 * gate) * (up + 1.0)
            term = nn_dot(activated.astype(jnp.bfloat16), down_ref[here])
            added = term if added is None else added + term

        @pl.when(i == 0)
        def _():
            total_ref[...] = added

        @pl.when(i > 0)
        def _():
            total_ref[...] += added

        return carry

    lax.fori_loop(0, down_refs[0].shape[0] // tile, add_tile, 0)
    for d, out_ref in enumerate(out_refs):
        out_ref[...] = total_ref[d * capacity : (d + 1) * capacity].astype(jnp.bfloat16)


def expert(rows, gate_ups, downs, after):
    ctx_count = len(rows)
    capacity, columns = rows[0].shape
    tile = downs[0].shape[0] // 3
    return pl.pallas_call(
        functools.partial(expert_kernel, ctx_count, tile),
        out_shape=[jax.ShapeDtypeStruct((capacity, columns), jnp.bfloat16)] * ctx_count,
        in_specs=[VMEM_SPEC] * (ctx_count + 4) + [ANY_SPEC] * len(after),
        out_specs=[VMEM_SPEC] * ctx_count,
        scratch_shapes=[pltpu.VMEM((ctx_count * capacity, columns), jnp.float32)],
        compiler_params=pltpu.CompilerParams(vmem_limit_bytes=16 << 20),
        cost_estimate=SMALL_COST,
    )(*rows, *gate_ups, *downs, *after)


def mix_kernel(ctx_count, extra_count, mix_ref, *refs):
    back_refs, extra_refs = refs[:ctx_count], refs[ctx_count : ctx_count + extra_count]
    out_ref = refs[-1]
    back = jnp.concatenate([back_ref[...] for back_ref in back_refs], axis=0)
    total = nn_dot(mix_ref[...], back)
    for extra_ref in extra_refs:
        total = total + merged(extra_ref[...]).astype(jnp.float32)
    out_ref[...] = total.astype(out_ref.dtype).reshape(out_ref.shape)


def mix_rows(mix, back, extra, after, dtype=jnp.bfloat16):
    tokens, count = mix.shape
    columns = back[0].shape[1]
    shape = (2, tokens // 2, columns)
    return pl.pallas_call(
        functools.partial(mix_kernel, len(back), len(extra)),
        out_shape=jax.ShapeDtypeStruct(shape, dtype),
        in_specs=[VMEM_SPEC] * (1 + len(back) + len(extra)) + [ANY_SPEC] * len(after),
        out_specs=VMEM_SPEC,
        compiler_params=pltpu.CompilerParams(vmem_limit_bytes=8 << 20),
        cost_estimate=SMALL_COST,
    )(mix, *back, *extra, *after)


def sum_kernel(part_count, *refs):
    total = refs[0][...]
    for part_ref in refs[1:part_count]:
        total = total + part_ref[...].astype(jnp.float32)
    refs[-1][...] = total.astype(jnp.bfloat16)


def sum_parts(parts, after):
    return pl.pallas_call(
        functools.partial(sum_kernel, len(parts)),
        out_shape=jax.ShapeDtypeStruct(parts[0].shape, jnp.bfloat16),
        in_specs=[VMEM_SPEC] * len(parts) + [ANY_SPEC] * len(after),
        out_specs=VMEM_SPEC,
        compiler_params=pltpu.CompilerParams(vmem_limit_bytes=4 << 20),
        cost_estimate=SMALL_COST,
    )(*parts, *after)


def local(
    queries,
    key_rows,
    value_matrix,
    hidden,
    out_weight,
    norm_gain,
    block_order,
    expert_ids,
    route_weights,
    gate_up_weight,
    down_weight,
):
    ctx_count = lax.axis_size("ctx")
    planes = lax.axis_size("exp") // 2
    ctx_scalar = lax.axis_index("ctx").astype(jnp.int32).reshape(1)
    plane_index = (lax.axis_index("exp") // 2).astype(jnp.int32)
    plane_scalars = jnp.stack([plane_index, jnp.full_like(plane_index, planes)])
    token_count = queries.shape[1]
    experts = ctx_count * planes
    capacity = 2 * token_count * TOPK // experts
    last = ctx_count - 1

    packed = pack(ctx_scalar, queries[0], key_rows[0], value_matrix[0], ctx_count)
    got = [ctx_swap(packed[d], d) for d in range(ctx_count)]

    gate_up_mine = jnp.swapaxes(gate_up_weight[0], 0, 1)
    down_mine = down_weight[0]
    half = down_mine.shape[0]
    got, gate_up_mine, down_mine = lax.optimization_barrier((got, gate_up_mine, down_mine))

    weight = jnp.swapaxes(out_weight, 0, 1)
    partners = tuple(range(last, 0, -1))
    parts = list(attend(partners, ctx_scalar, block_order, weight, got, None, []))
    swapped = [core_swap(gate_up_mine), core_swap(down_mine)]
    hidden_columns = jnp.swapaxes(hidden[0], 0, 1)
    own = attend((0,), ctx_scalar, block_order, weight, got, hidden_columns, parts[:1])
    parts = [ctx_swap(part, last - i) for i, part in enumerate(parts)]
    other = [copy_after(w, list(own)) for w in swapped]
    gate_ups = [w.reshape(2, half, D) for w in (gate_up_mine, other[0])]
    downs = [down_mine, other[1]]

    route = jnp.concatenate(
        [expert_ids[0].astype(jnp.bfloat16), route_weights[0].astype(jnp.bfloat16)], axis=1
    )
    route = jnp.pad(route, ((0, 0), (0, -D % 128 - 2 * TOPK)))
    residual, held, mix, *rows = norm_and_pick(
        ctx_scalar, plane_scalars, norm_gain[None], route, list(own) + parts, capacity, other
    )

    def spread(blocks):
        return [ctx_swap(blocks[d], d) for d in range(ctx_count)]

    mixes = [mix]
    arrived = [spread(rows)]
    back = [None] * planes

    def run_expert(s, after):
        result = expert(arrived[s], gate_ups, downs, after)
        if s > 0:
            back[s] = spread(result)
        return list(result)

    def run_mix(s, carried, after):
        part = mix_rows(mixes[s], back[s], carried, after)
        return [part], [plane_shift(part, 1)]

    done, carried = [], []
    for s in range(1, planes):
        held = plane_shift(held, 1)
        mix, *rows = pick_rows(ctx_scalar, plane_scalars, held, rows, arrived[s - 1][1:] + done[:1])
        held, rows = lax.optimization_barrier((held, rows))
        mixes.append(mix)
        arrived.append(spread(rows))
        done = run_expert(s - 1, list(rows[:1]))
        if s == 1:
            own_result = done
        if s > 2:
            done, carried = run_mix(s - 2, carried, done)
    done = run_expert(planes - 1, done)
    own_result, _ = lax.optimization_barrier((own_result, done))
    back[0] = spread(own_result)
    for s in range(max(planes - 2, 1), planes):
        done, carried = run_mix(s, carried, done)
    own = mix_rows(mixes[0], back[0], [residual], done, jnp.float32)
    out = sum_parts([own] + carried, [])
    return out.reshape(1, token_count, D)


def solution(mesh):
    return jax.shard_map(
        local,
        mesh=mesh,
        in_specs=(
            P("exp", "ctx", None),
            P("exp", "ctx", None),
            P("exp", "ctx", None),
            P("exp", "ctx", None),
            P("ctx", None),
            P(),
            P(),
            P("exp", "ctx", None),
            P("exp", "ctx", None),
            P(("ctx", "exp"), None, None),
            P(("ctx", "exp"), None, None),
        ),
        out_specs=P("exp", "ctx", None),
        check_vma=False,
    )
```

```python
import functools

import jax
import jax.numpy as jnp
from jax import lax
from jax.experimental import pallas as pl
from jax.experimental.pallas import tpu as pltpu
from jax.sharding import PartitionSpec as P

D = 2880
QUERY_HEADS = 32
KEY_VALUE_HEADS = 4
HEAD_SIZE = 64
TOPK = 4


negative_large = -1e30


def ctx_swap(rows, distance):
    if distance == 0:
        return rows
    count = lax.axis_size("ctx")
    return lax.ppermute(rows, "ctx", [(i, i ^ distance) for i in range(count)])


def plane_shift(rows, planes):
    count = lax.axis_size("exp")
    if (2 * planes) % count == 0:
        return rows
    return lax.ppermute(rows, "exp", [(i, (i + 2 * planes) % count) for i in range(count)])


def core_swap(rows):
    count = lax.axis_size("exp")
    return lax.ppermute(rows, "exp", [(i, i ^ 1) for i in range(count)])

ANY_SPEC = pl.BlockSpec(memory_space=pl.ANY)
SMEM_SPEC = pl.BlockSpec(memory_space=pltpu.SMEM)
VMEM_SPEC = pl.BlockSpec(memory_space=pltpu.VMEM)
SMALL_COST = pl.CostEstimate(flops=1, bytes_accessed=1, transcendentals=0)


def nt_dot(left, right):
    return lax.dot_general(
        left, right, (((1,), (1,)), ((), ())), preferred_element_type=jnp.float32
    )


def nn_dot(left, right):
    return jnp.dot(left, right, preferred_element_type=jnp.float32)


def merged(block):
    return block.reshape(block.shape[0] * block.shape[1], block.shape[2])


def start_copies(pairs, sems, first=0):
    copies = [
        pltpu.make_async_copy(source, target, sems.at[first + i])
        for i, (source, target) in enumerate(pairs)
    ]
    for copy in copies:
        copy.start()
    return copies


def pack_kernel(ctx_count, ctx_ref, q_ref, k_ref, v_ref, *refs):
    out_refs, (q_buf, k_buf, v_buf, sems) = refs[:ctx_count], refs[ctx_count:]
    heads_here = QUERY_HEADS // ctx_count
    group = QUERY_HEADS // KEY_VALUE_HEADS
    width = heads_here * HEAD_SIZE
    rows = q_ref.shape[0]
    for copy in start_copies([(k_ref, k_buf), (v_ref, v_buf), (q_ref, q_buf)], sems):
        copy.wait()
    low = lax.broadcasted_iota(jnp.int32, (rows, 2 * HEAD_SIZE), 1) < HEAD_SIZE
    for d in range(ctx_count):
        to = ctx_ref[0] ^ d
        head = (to * heads_here) // group
        odd = (head % 2) == 1
        pair = pl.ds(pl.multiple_of((head // 2) * 2 * HEAD_SIZE, 2 * HEAD_SIZE), 2 * HEAD_SIZE)
        keys = k_buf[:, pair].astype(jnp.float32)
        values = v_buf[:, pair].astype(jnp.float32)
        keys = jnp.where(odd, pltpu.roll(keys, HEAD_SIZE, 1), keys)
        values = jnp.where(odd, values, pltpu.roll(values, HEAD_SIZE, 1))
        columns = pl.ds(pl.multiple_of(to * width, width), width)
        out_refs[d][:, :width] = q_buf[:, columns]
        out_refs[d][:, width:] = jnp.where(low, keys, values).astype(jnp.bfloat16)


def pack(ctx_scalar, queries, keys, values, ctx_count):
    rows, width = queries.shape[0], queries.shape[1] // ctx_count
    shape = jax.ShapeDtypeStruct((rows, width + 2 * HEAD_SIZE), jnp.bfloat16)
    return pl.pallas_call(
        functools.partial(pack_kernel, ctx_count),
        out_shape=[shape] * ctx_count,
        in_specs=[SMEM_SPEC] + [ANY_SPEC] * 3,
        out_specs=[VMEM_SPEC] * ctx_count,
        scratch_shapes=[pltpu.VMEM(x.shape, x.dtype) for x in (queries, keys, values)]
        + [pltpu.SemaphoreType.DMA((3,))],
        compiler_params=pltpu.CompilerParams(vmem_limit_bytes=56 << 20),
        cost_estimate=SMALL_COST,
    )(ctx_scalar, queries, keys, values)


def copy_kernel(source_ref, *refs):
    refs[-1][...] = source_ref[...]


def copy_after(source, after):
    return pl.pallas_call(
        copy_kernel,
        out_shape=jax.ShapeDtypeStruct(source.shape, source.dtype),
        in_specs=[VMEM_SPEC] + [ANY_SPEC] * len(after),
        out_specs=VMEM_SPEC,
        compiler_params=pltpu.CompilerParams(vmem_limit_bytes=20 << 20),
        cost_estimate=SMALL_COST,
    )(source, *after)


def attend_kernel(dests, ctx_count, ctx_ref, order_ref, weight_ref, *refs):
    out_refs, (weight_buf, got_refs, sems) = refs[-3 - len(dests) : -3], refs[-3:]
    hidden_ref, arrived_ref = refs[ctx_count : ctx_count + 2]
    copies = start_copies([(refs[d], got_refs.at[d]) for d in range(ctx_count)], sems)
    weight_copy = start_copies([(weight_ref, weight_buf)], sems, ctx_count)[0]
    for copy in copies:
        copy.wait()
    heads_here = QUERY_HEADS // ctx_count
    width = heads_here * HEAD_SIZE
    rows = got_refs.shape[1]
    block = rows // 2
    me = ctx_ref[0]
    lanes = lax.broadcasted_iota(jnp.int32, (rows, 2 * HEAD_SIZE), 1) < HEAD_SIZE
    keys, values, key_pos = [], [], []
    place = lax.broadcasted_iota(jnp.int32, (1, rows), 1)
    for d in range(ctx_count):
        both = got_refs[d, :, width:].astype(jnp.float32)
        other = pltpu.roll(both, HEAD_SIZE, 1)
        scaled = jnp.where(lanes, both, other) * HEAD_SIZE ** (-0.5)
        keys.append(scaled.astype(jnp.bfloat16))
        values.append(jnp.where(lanes, other, both).astype(jnp.bfloat16))
        slot = 2 * (me ^ d)
        first, second = order_ref[slot] * block, order_ref[slot + 1] * block - block
        key_pos.append(place + jnp.where(place < block, first, second))
    keys = jnp.concatenate(keys, axis=0)
    values = jnp.concatenate(values, axis=0)
    key_pos = jnp.concatenate(key_pos, axis=1)
    row = lax.broadcasted_iota(jnp.int32, (rows, 1), 0)
    stacked, visible, attended = [], [], []
    for d in dests:
        slot = 2 * (me ^ d)
        first, second = order_ref[slot] * block, order_ref[slot + 1] * block - block
        query_pos = row + jnp.where(row < block, first, second)
        visible += [key_pos <= query_pos] * heads_here
        for pair in range(heads_here // 2):
            both = got_refs[d, :, pair * 2 * HEAD_SIZE : (pair + 1) * 2 * HEAD_SIZE]
            for side in range(2):
                stacked.append(jnp.where(lanes == (side == 0), both, jnp.zeros_like(both)))
    scores = nt_dot(jnp.concatenate(stacked, axis=0), keys)
    scores = jnp.where(jnp.concatenate(visible, axis=0), scores, negative_large)
    probs = jnp.exp(scores - jnp.max(scores, axis=-1, keepdims=True))
    total = jnp.sum(probs, axis=-1, keepdims=True)
    mixed = nn_dot(probs.astype(jnp.bfloat16), values) / total
    mixed = [mixed[i * rows : (i + 1) * rows] for i in range(len(stacked))]
    for i in range(len(dests)):
        pairs = []
        for head in range(i * heads_here, (i + 1) * heads_here, 2):
            pairs.append(jnp.where(lanes, mixed[head], mixed[head + 1]).astype(jnp.bfloat16))
        attended.append(jnp.concatenate(pairs, axis=1))
    weight_copy.wait()
    parts = nt_dot(jnp.concatenate(attended, axis=0), weight_buf[...])
    for i, (out_ref, d) in enumerate(zip(out_refs, dests)):
        part = parts[i * rows : (i + 1) * rows]
        if d == 0:
            eye = lax.broadcasted_iota(jnp.int32, (rows, rows), 1) == row
            part = part + nt_dot(eye.astype(jnp.bfloat16), hidden_ref[...])
            part = part + merged(arrived_ref[...]).astype(jnp.float32)
        out_ref[...] = part.astype(out_ref.dtype).reshape(out_ref.shape)


def attend(dests, ctx_scalar, order, weight, got, added, after):
    ctx_count = len(got)
    rows, columns = got[0].shape[0], weight.shape[0]
    shapes = [
        jax.ShapeDtypeStruct((2, rows // 2, columns), jnp.bfloat16 if d else jnp.float32)
        for d in dests
    ]
    work = len(dests) * rows * weight.shape[1]
    return pl.pallas_call(
        functools.partial(attend_kernel, dests, ctx_count),
        out_shape=shapes,
        in_specs=[SMEM_SPEC, SMEM_SPEC]
        + [ANY_SPEC] * (1 + ctx_count)
        + [VMEM_SPEC] * len(added)
        + [ANY_SPEC] * len(after),
        out_specs=[VMEM_SPEC] * len(dests),
        scratch_shapes=[
            pltpu.VMEM(weight.shape, weight.dtype),
            pltpu.VMEM((ctx_count,) + got[0].shape, got[0].dtype),
            pltpu.SemaphoreType.DMA((ctx_count + 1,)),
        ],
        compiler_params=pltpu.CompilerParams(vmem_limit_bytes=56 << 20),
        cost_estimate=SMALL_COST,
    )(ctx_scalar, order, weight, *got, *added, *after)


def pick_and_mix(ctx_count, capacity, ctx_ref, plane_ref, held, route, out_refs, mix_ref):
    tokens = held.shape[0]
    count = ctx_count * capacity
    lane = lax.broadcasted_iota(jnp.int32, (1, count), 1)
    partner = ctx_ref[0] ^ (lane // capacity)
    wanted = (partner * plane_ref[1] + plane_ref[0]).astype(jnp.float32)
    member = jnp.zeros((tokens, count), jnp.float32)
    weight = jnp.zeros((tokens, count), jnp.float32)
    for k in range(TOPK):
        chosen = route[:, k : k + 1] == wanted
        member = jnp.where(chosen, 1.0, member)
        weight = jnp.where(chosen, route[:, TOPK + k : TOPK + k + 1], weight)
    row = lax.broadcasted_iota(jnp.int32, (tokens, tokens), 0)
    earlier = lax.broadcasted_iota(jnp.int32, (tokens, tokens), 1) < row
    rank = nn_dot(earlier.astype(jnp.bfloat16), member.astype(jnp.bfloat16))
    slot = (lane % capacity).astype(jnp.float32)
    placed = jnp.where(rank == slot, member, 0.0)
    mix_ref[...] = (placed * weight).astype(jnp.bfloat16)
    picked = nn_dot(placed.T.astype(jnp.bfloat16), held).astype(jnp.bfloat16)
    for d, out_ref in enumerate(out_refs):
        out_ref[...] = picked[d * capacity : (d + 1) * capacity]


def norm_kernel(ctx_count, part_count, ctx_ref, plane_ref, gain_ref, route_ref, *refs):
    part_refs = refs[:part_count]
    residual_ref, normed_ref, mix_ref, *out_refs = refs[-3 - ctx_count :]
    capacity, columns = out_refs[0].shape
    total = merged(part_refs[0][...])
    for part_ref in part_refs[1:]:
        total = total + merged(part_ref[...]).astype(jnp.float32)
    residual = total.astype(jnp.bfloat16)
    residual_ref[...] = residual.reshape(residual_ref.shape)
    res_float = residual.astype(jnp.float32)
    mean = jnp.mean(res_float * res_float, axis=-1, keepdims=True)
    normed = (res_float * lax.rsqrt(mean + 1e-05) * gain_ref[...]).astype(jnp.bfloat16)
    route = route_ref[...]
    normed_ref[:, :, :columns] = normed.reshape(residual_ref.shape)
    normed_ref[:, :, columns:] = route.reshape(normed_ref.shape[:2] + route.shape[1:])
    pick_and_mix(
        ctx_count,
        capacity,
        ctx_ref,
        plane_ref,
        normed,
        route.astype(jnp.float32),
        out_refs,
        mix_ref,
    )


def pick_shapes(ctx_count, capacity, tokens, columns):
    slot = jax.ShapeDtypeStruct((capacity, columns), jnp.bfloat16)
    return [jax.ShapeDtypeStruct((tokens, ctx_count * capacity), jnp.bfloat16)] + [slot] * ctx_count


def norm_and_pick(ctx_scalar, plane_scalars, gain, route, parts, ctx_count, capacity, after):
    _, half, columns = parts[0].shape
    tokens, extra = route.shape
    return pl.pallas_call(
        functools.partial(norm_kernel, ctx_count, len(parts)),
        out_shape=[
            jax.ShapeDtypeStruct((2, half, columns), jnp.bfloat16),
            jax.ShapeDtypeStruct((2, half, columns + extra), jnp.bfloat16),
        ]
        + pick_shapes(ctx_count, capacity, tokens, columns),
        in_specs=[SMEM_SPEC] * 2 + [VMEM_SPEC] * (2 + len(parts)) + [ANY_SPEC] * len(after),
        out_specs=[VMEM_SPEC] * (3 + ctx_count),
        compiler_params=pltpu.CompilerParams(vmem_limit_bytes=12 << 20),
        cost_estimate=SMALL_COST,
    )(ctx_scalar, plane_scalars, gain, route, *parts, *after)


def pick_kernel(ctx_count, ctx_ref, plane_ref, held_ref, *refs):
    mix_ref, *out_refs = refs[-1 - ctx_count :]
    capacity, columns = out_refs[0].shape
    held = merged(held_ref[:, :, :columns])
    route = merged(held_ref[:, :, columns:]).astype(jnp.float32)
    pick_and_mix(ctx_count, capacity, ctx_ref, plane_ref, held, route, out_refs, mix_ref)


def pick_rows(ctx_scalar, plane_scalars, held, like, after):
    ctx_count = len(like)
    capacity, columns = like[0].shape
    return pl.pallas_call(
        functools.partial(pick_kernel, ctx_count),
        out_shape=pick_shapes(ctx_count, capacity, 2 * held.shape[1], columns),
        in_specs=[SMEM_SPEC] * 2 + [VMEM_SPEC] + [ANY_SPEC] * len(after),
        out_specs=[VMEM_SPEC] * (1 + ctx_count),
        compiler_params=pltpu.CompilerParams(vmem_limit_bytes=6 << 20),
        cost_estimate=SMALL_COST,
    )(ctx_scalar, plane_scalars, held, *after)


def expert_kernel(ctx_count, tile, *refs):
    row_refs, refs = refs[:ctx_count], refs[ctx_count:]
    gate_up_refs, down_refs = refs[:2], refs[2:4]
    out_refs, total_ref = refs[-ctx_count - 1 : -1], refs[-1]
    capacity = row_refs[0].shape[0]

    def add_tile(i, carry):
        routed = jnp.concatenate([row_ref[...] for row_ref in row_refs], axis=0)
        here = pl.ds(pl.multiple_of(i * tile, tile), tile)
        added = None
        for gate_up_ref, down_ref in zip(gate_up_refs, down_refs):
            gate = nt_dot(routed, gate_up_ref[0, here])
            up = nt_dot(routed, gate_up_ref[1, here])
            activated = gate * jax.nn.sigmoid(1.702 * gate) * (up + 1.0)
            term = nn_dot(activated.astype(jnp.bfloat16), down_ref[here])
            added = term if added is None else added + term

        @pl.when(i == 0)
        def _():
            total_ref[...] = added

        @pl.when(i > 0)
        def _():
            total_ref[...] += added

        return carry

    lax.fori_loop(0, down_refs[0].shape[0] // tile, add_tile, 0)
    for d, out_ref in enumerate(out_refs):
        out_ref[...] = total_ref[d * capacity : (d + 1) * capacity].astype(jnp.bfloat16)


def expert(rows, gate_ups, downs, after, tiles):
    ctx_count = len(rows)
    capacity, columns = rows[0].shape
    tile = downs[0].shape[0] // tiles
    return pl.pallas_call(
        functools.partial(expert_kernel, ctx_count, tile),
        out_shape=[jax.ShapeDtypeStruct((capacity, columns), jnp.bfloat16)] * ctx_count,
        in_specs=[VMEM_SPEC] * (ctx_count + 4) + [ANY_SPEC] * len(after),
        out_specs=[VMEM_SPEC] * ctx_count,
        scratch_shapes=[pltpu.VMEM((ctx_count * capacity, columns), jnp.float32)],
        compiler_params=pltpu.CompilerParams(vmem_limit_bytes=16 << 20),
        cost_estimate=SMALL_COST,
    )(*rows, *gate_ups, *downs, *after)


def mix_kernel(ctx_count, extra_count, mix_ref, *refs):
    back_refs, extra_refs = refs[:ctx_count], refs[ctx_count : ctx_count + extra_count]
    out_ref = refs[-1]
    back = jnp.concatenate([back_ref[...] for back_ref in back_refs], axis=0)
    total = nn_dot(mix_ref[...], back)
    for extra_ref in extra_refs:
        total = total + merged(extra_ref[...]).astype(jnp.float32)
    out_ref[...] = total.astype(out_ref.dtype).reshape(out_ref.shape)


def mix_rows(mix, back, extra, after, dtype=jnp.bfloat16):
    tokens, count = mix.shape
    columns = back[0].shape[1]
    shape = (2, tokens // 2, columns)
    return pl.pallas_call(
        functools.partial(mix_kernel, len(back), len(extra)),
        out_shape=jax.ShapeDtypeStruct(shape, dtype),
        in_specs=[VMEM_SPEC] * (1 + len(back) + len(extra)) + [ANY_SPEC] * len(after),
        out_specs=VMEM_SPEC,
        compiler_params=pltpu.CompilerParams(vmem_limit_bytes=8 << 20),
        cost_estimate=SMALL_COST,
    )(mix, *back, *extra, *after)


def sum_kernel(part_count, *refs):
    total = refs[0][...]
    for part_ref in refs[1:part_count]:
        total = total + part_ref[...].astype(jnp.float32)
    refs[-1][...] = total.astype(jnp.bfloat16)


def sum_parts(parts, after):
    return pl.pallas_call(
        functools.partial(sum_kernel, len(parts)),
        out_shape=jax.ShapeDtypeStruct(parts[0].shape, jnp.bfloat16),
        in_specs=[VMEM_SPEC] * len(parts) + [ANY_SPEC] * len(after),
        out_specs=VMEM_SPEC,
        compiler_params=pltpu.CompilerParams(vmem_limit_bytes=4 << 20),
        cost_estimate=SMALL_COST,
    )(*parts, *after)


def local(
    queries,
    key_rows,
    value_matrix,
    hidden,
    out_weight,
    norm_gain,
    block_order,
    expert_ids,
    route_weights,
    gate_up_weight,
    down_weight,
):
    ctx_count = lax.axis_size("ctx")
    planes = lax.axis_size("exp") // 2
    ctx_scalar = lax.axis_index("ctx").astype(jnp.int32).reshape(1)
    plane_index = (lax.axis_index("exp") // 2).astype(jnp.int32)
    plane_scalars = jnp.stack([plane_index, jnp.full_like(plane_index, planes)])
    token_count = queries.shape[1]
    experts = ctx_count * planes
    capacity = 2 * token_count * TOPK // experts
    last = ctx_count - 1

    packed = pack(ctx_scalar, queries[0], key_rows[0], value_matrix[0], ctx_count)
    got = [ctx_swap(packed[d], d) for d in range(ctx_count)]

    gate_up_mine = jnp.swapaxes(gate_up_weight[0], 0, 1)
    down_mine = down_weight[0]
    half = down_mine.shape[0]
    got, gate_up_mine, down_mine = lax.optimization_barrier((got, gate_up_mine, down_mine))

    weight = jnp.swapaxes(out_weight, 0, 1)
    first = list(attend((last,), ctx_scalar, block_order, weight, got, [], []))
    partners = tuple(range(last - 1, 0, -1))
    parts = list(attend(partners, ctx_scalar, block_order, weight, got, [], first))
    swapped = [core_swap(gate_up_mine), core_swap(down_mine)]
    hidden_columns = jnp.swapaxes(hidden[0], 0, 1)
    added = [hidden_columns, ctx_swap(first[0], last)]
    own = attend((0,), ctx_scalar, block_order, weight, got, added, parts[:1])
    parts = [ctx_swap(part, partners[i]) for i, part in enumerate(parts)]
    other = [copy_after(w, list(own)) for w in swapped]
    gate_ups = [w.reshape(2, half, D) for w in (gate_up_mine, other[0])]
    downs = [down_mine, other[1]]

    route = jnp.concatenate(
        [expert_ids[0].astype(jnp.bfloat16), route_weights[0].astype(jnp.bfloat16)], axis=1
    )
    route = jnp.pad(route, ((0, 0), (0, -D % 128 - 2 * TOPK)))
    residual, held, mix, *rows = norm_and_pick(
        ctx_scalar,
        plane_scalars,
        norm_gain[None],
        route,
        list(own) + parts,
        ctx_count,
        capacity,
        other,
    )

    def spread(blocks):
        return [ctx_swap(blocks[d], d) for d in range(ctx_count)]

    mixes = [mix]
    arrived = [spread(rows)]
    back = [None] * planes

    def run_expert(s, after):
        result = expert(arrived[s], gate_ups, downs, after, 1 if s == planes - 1 else 3)
        if s > 0:
            back[s] = spread(result)
        return list(result)

    def run_mix(s, carried, after):
        part = mix_rows(mixes[s], back[s], carried, after)
        return [part], [plane_shift(part, 1)]

    done, carried = [], []
    for s in range(1, planes):
        held = plane_shift(held, 1)
        mix, *rows = pick_rows(ctx_scalar, plane_scalars, held, rows, arrived[s - 1][1:] + done[:1])
        held, rows = lax.optimization_barrier((held, rows))
        mixes.append(mix)
        arrived.append(spread(rows))
        done = run_expert(s - 1, list(rows[:1]))
        if s == 1:
            own_result = done
        if s > 2:
            done, carried = run_mix(s - 2, carried, done)
    done = run_expert(planes - 1, done)
    own_result, _ = lax.optimization_barrier((own_result, done))
    back[0] = spread(own_result)
    for s in range(max(planes - 2, 1), planes):
        done, carried = run_mix(s, carried, done)
    own = mix_rows(mixes[0], back[0], [residual], done, jnp.float32)
    out = sum_parts([own] + carried, [])
    return out.reshape(1, token_count, D)


def solution(mesh):
    return jax.shard_map(
        local,
        mesh=mesh,
        in_specs=(
            P("exp", "ctx", None),
            P("exp", "ctx", None),
            P("exp", "ctx", None),
            P("exp", "ctx", None),
            P("ctx", None),
            P(),
            P(),
            P("exp", "ctx", None),
            P("exp", "ctx", None),
            P(("ctx", "exp"), None, None),
            P(("ctx", "exp"), None, None),
        ),
        out_specs=P("exp", "ctx", None),
        check_vma=False,
    )
```

```python
import functools

import jax
import jax.numpy as jnp
from jax import lax
from jax.experimental import pallas as pl
from jax.experimental.pallas import tpu as pltpu
from jax.sharding import PartitionSpec as P

D = 2880
QUERY_HEADS = 32
KEY_VALUE_HEADS = 4
HEAD_SIZE = 64
TOPK = 4


negative_large = -1e30


def ctx_swap(rows, distance):
    if distance == 0:
        return rows
    count = lax.axis_size("ctx")
    return lax.ppermute(rows, "ctx", [(i, i ^ distance) for i in range(count)])


def plane_shift(rows, planes):
    count = lax.axis_size("exp")
    if (2 * planes) % count == 0:
        return rows
    return lax.ppermute(rows, "exp", [(i, (i + 2 * planes) % count) for i in range(count)])


def core_swap(rows):
    count = lax.axis_size("exp")
    return lax.ppermute(rows, "exp", [(i, i ^ 1) for i in range(count)])

ANY_SPEC = pl.BlockSpec(memory_space=pl.ANY)
SMEM_SPEC = pl.BlockSpec(memory_space=pltpu.SMEM)
VMEM_SPEC = pl.BlockSpec(memory_space=pltpu.VMEM)
SMALL_COST = pl.CostEstimate(flops=1, bytes_accessed=1, transcendentals=0)


def nt_dot(left, right):
    return lax.dot_general(
        left, right, (((1,), (1,)), ((), ())), preferred_element_type=jnp.float32
    )


def nn_dot(left, right):
    return jnp.dot(left, right, preferred_element_type=jnp.float32)


def merged(block):
    return block.reshape(block.shape[0] * block.shape[1], block.shape[2])


def start_copies(pairs, sems, first=0):
    copies = [
        pltpu.make_async_copy(source, target, sems.at[first + i])
        for i, (source, target) in enumerate(pairs)
    ]
    for copy in copies:
        copy.start()
    return copies


def pack_kernel(ctx_count, ctx_ref, q_ref, k_ref, v_ref, *refs):
    out_refs, (q_buf, k_buf, v_buf, sems) = refs[:ctx_count], refs[ctx_count:]
    heads_here = QUERY_HEADS // ctx_count
    group = QUERY_HEADS // KEY_VALUE_HEADS
    width = heads_here * HEAD_SIZE
    rows = q_ref.shape[0]
    for copy in start_copies([(k_ref, k_buf), (v_ref, v_buf), (q_ref, q_buf)], sems):
        copy.wait()
    low = lax.broadcasted_iota(jnp.int32, (rows, 2 * HEAD_SIZE), 1) < HEAD_SIZE
    for d in range(ctx_count):
        to = ctx_ref[0] ^ d
        head = (to * heads_here) // group
        odd = (head % 2) == 1
        pair = pl.ds(pl.multiple_of((head // 2) * 2 * HEAD_SIZE, 2 * HEAD_SIZE), 2 * HEAD_SIZE)
        keys = k_buf[:, pair].astype(jnp.float32)
        values = v_buf[:, pair].astype(jnp.float32)
        keys = jnp.where(odd, pltpu.roll(keys, HEAD_SIZE, 1), keys)
        values = jnp.where(odd, values, pltpu.roll(values, HEAD_SIZE, 1))
        columns = pl.ds(pl.multiple_of(to * width, width), width)
        out_refs[d][:, :width] = q_buf[:, columns]
        out_refs[d][:, width:] = jnp.where(low, keys, values).astype(jnp.bfloat16)


def pack(ctx_scalar, queries, keys, values, ctx_count):
    rows, width = queries.shape[0], queries.shape[1] // ctx_count
    shape = jax.ShapeDtypeStruct((rows, width + 2 * HEAD_SIZE), jnp.bfloat16)
    return pl.pallas_call(
        functools.partial(pack_kernel, ctx_count),
        out_shape=[shape] * ctx_count,
        in_specs=[SMEM_SPEC] + [ANY_SPEC] * 3,
        out_specs=[VMEM_SPEC] * ctx_count,
        scratch_shapes=[pltpu.VMEM(x.shape, x.dtype) for x in (queries, keys, values)]
        + [pltpu.SemaphoreType.DMA((3,))],
        compiler_params=pltpu.CompilerParams(vmem_limit_bytes=56 << 20),
        cost_estimate=SMALL_COST,
    )(ctx_scalar, queries, keys, values)


def copy_kernel(source_ref, *refs):
    refs[-1][...] = source_ref[...]


def copy_after(source, after):
    return pl.pallas_call(
        copy_kernel,
        out_shape=jax.ShapeDtypeStruct(source.shape, source.dtype),
        in_specs=[VMEM_SPEC] + [ANY_SPEC] * len(after),
        out_specs=VMEM_SPEC,
        compiler_params=pltpu.CompilerParams(vmem_limit_bytes=20 << 20),
        cost_estimate=SMALL_COST,
    )(source, *after)


def attend_kernel(dests, ctx_count, ctx_ref, order_ref, weight_ref, *refs):
    out_refs, (weight_buf, got_refs, sems) = refs[-3 - len(dests) : -3], refs[-3:]
    hidden_ref, arrived_ref = refs[ctx_count : ctx_count + 2]
    copies = start_copies([(refs[d], got_refs.at[d]) for d in range(ctx_count)], sems)
    weight_copy = start_copies([(weight_ref, weight_buf)], sems, ctx_count)[0]
    for copy in copies:
        copy.wait()
    heads_here = QUERY_HEADS // ctx_count
    width = heads_here * HEAD_SIZE
    rows = got_refs.shape[1]
    block = rows // 2
    me = ctx_ref[0]
    lanes = lax.broadcasted_iota(jnp.int32, (rows, 2 * HEAD_SIZE), 1) < HEAD_SIZE
    keys, values, key_pos = [], [], []
    place = lax.broadcasted_iota(jnp.int32, (1, rows), 1)
    for d in range(ctx_count):
        both = got_refs[d, :, width:].astype(jnp.float32)
        other = pltpu.roll(both, HEAD_SIZE, 1)
        scaled = jnp.where(lanes, both, other) * HEAD_SIZE ** (-0.5)
        keys.append(scaled.astype(jnp.bfloat16))
        values.append(jnp.where(lanes, other, both).astype(jnp.bfloat16))
        slot = 2 * (me ^ d)
        first, second = order_ref[slot] * block, order_ref[slot + 1] * block - block
        key_pos.append(place + jnp.where(place < block, first, second))
    keys = jnp.concatenate(keys, axis=0)
    values = jnp.concatenate(values, axis=0)
    key_pos = jnp.concatenate(key_pos, axis=1)
    row = lax.broadcasted_iota(jnp.int32, (rows, 1), 0)
    stacked, visible, attended = [], [], []
    for d in dests:
        slot = 2 * (me ^ d)
        first, second = order_ref[slot] * block, order_ref[slot + 1] * block - block
        query_pos = row + jnp.where(row < block, first, second)
        visible += [key_pos <= query_pos] * heads_here
        for pair in range(heads_here // 2):
            both = got_refs[d, :, pair * 2 * HEAD_SIZE : (pair + 1) * 2 * HEAD_SIZE]
            for side in range(2):
                stacked.append(jnp.where(lanes == (side == 0), both, jnp.zeros_like(both)))
    scores = nt_dot(jnp.concatenate(stacked, axis=0), keys)
    scores = jnp.where(jnp.concatenate(visible, axis=0), scores, negative_large)
    probs = jnp.exp(scores - jnp.max(scores, axis=-1, keepdims=True))
    total = jnp.sum(probs, axis=-1, keepdims=True)
    mixed = nn_dot(probs.astype(jnp.bfloat16), values) / total
    mixed = [mixed[i * rows : (i + 1) * rows] for i in range(len(stacked))]
    for i in range(len(dests)):
        pairs = []
        for head in range(i * heads_here, (i + 1) * heads_here, 2):
            pairs.append(jnp.where(lanes, mixed[head], mixed[head + 1]).astype(jnp.bfloat16))
        attended.append(jnp.concatenate(pairs, axis=1))
    weight_copy.wait()
    parts = nt_dot(jnp.concatenate(attended, axis=0), weight_buf[...])
    for i, (out_ref, d) in enumerate(zip(out_refs, dests)):
        part = parts[i * rows : (i + 1) * rows]
        if d == 0:
            eye = lax.broadcasted_iota(jnp.int32, (rows, rows), 1) == row
            part = part + nt_dot(eye.astype(jnp.bfloat16), hidden_ref[...])
            part = part + merged(arrived_ref[...]).astype(jnp.float32)
        out_ref[...] = part.astype(out_ref.dtype).reshape(out_ref.shape)


def attend(dests, ctx_scalar, order, weight, got, added, after):
    ctx_count = len(got)
    rows, columns = got[0].shape[0], weight.shape[0]
    shapes = [
        jax.ShapeDtypeStruct((2, rows // 2, columns), jnp.bfloat16 if d else jnp.float32)
        for d in dests
    ]
    work = len(dests) * rows * weight.shape[1]
    return pl.pallas_call(
        functools.partial(attend_kernel, dests, ctx_count),
        out_shape=shapes,
        in_specs=[SMEM_SPEC, SMEM_SPEC]
        + [ANY_SPEC] * (1 + ctx_count)
        + [VMEM_SPEC] * len(added)
        + [ANY_SPEC] * len(after),
        out_specs=[VMEM_SPEC] * len(dests),
        scratch_shapes=[
            pltpu.VMEM(weight.shape, weight.dtype),
            pltpu.VMEM((ctx_count,) + got[0].shape, got[0].dtype),
            pltpu.SemaphoreType.DMA((ctx_count + 1,)),
        ],
        compiler_params=pltpu.CompilerParams(vmem_limit_bytes=56 << 20),
        cost_estimate=SMALL_COST,
    )(ctx_scalar, order, weight, *got, *added, *after)


def mask_kernel(offsets, ctx_ref, plane_ref, *refs):
    sources, outs = refs[: len(offsets)], refs[-2 * len(offsets) :]
    for i, offset in enumerate(offsets):
        mix_ref, place_ref = outs[2 * i : 2 * i + 2]
        tokens, count = mix_ref.shape
        capacity = plane_ref[2]
        if len(sources[i].shape) == 3:
            route = merged(sources[i][:, :, D - D % 128 :]).astype(jnp.float32)
            offset = offset + D % 128
        else:
            route = sources[i][...].astype(jnp.float32)
        lane = lax.broadcasted_iota(jnp.int32, (1, count), 1)
        partner = ctx_ref[0] ^ (lane // capacity)
        wanted = (partner * plane_ref[1] + plane_ref[0]).astype(jnp.float32)
        member = jnp.zeros((tokens, count), jnp.float32)
        weight = jnp.zeros((tokens, count), jnp.float32)
        for k in range(offset, offset + TOPK):
            chosen = route[:, k : k + 1] == wanted
            member = jnp.where(chosen, 1.0, member)
            weight = jnp.where(chosen, route[:, TOPK + k : TOPK + k + 1], weight)
        row = lax.broadcasted_iota(jnp.int32, (tokens, tokens), 0)
        earlier = lax.broadcasted_iota(jnp.int32, (tokens, tokens), 1) < row
        rank = nn_dot(earlier.astype(jnp.bfloat16), member.astype(jnp.bfloat16))
        slot = (lane % capacity).astype(jnp.float32)
        placed = jnp.where(rank == slot, member, 0.0)
        mix_ref[...] = (placed * weight).astype(jnp.bfloat16)
        place_ref[...] = placed.T.astype(jnp.bfloat16)


def masks(ctx_scalar, plane_scalars, sources, offsets, tokens, count):
    shapes = [
        jax.ShapeDtypeStruct((tokens, count), jnp.bfloat16),
        jax.ShapeDtypeStruct((count, tokens), jnp.bfloat16),
    ]
    return pl.pallas_call(
        functools.partial(mask_kernel, offsets),
        out_shape=shapes * len(offsets),
        in_specs=[SMEM_SPEC] * 2 + [VMEM_SPEC] * len(offsets),
        out_specs=[VMEM_SPEC] * (2 * len(offsets)),
        compiler_params=pltpu.CompilerParams(vmem_limit_bytes=6 << 20),
        cost_estimate=SMALL_COST,
    )(ctx_scalar, plane_scalars, *sources)


def put_slots(place_ref, held, out_refs):
    capacity = out_refs[0].shape[0]
    picked = nn_dot(place_ref[...], held).astype(jnp.bfloat16)
    for d, out_ref in enumerate(out_refs):
        out_ref[...] = picked[d * capacity : (d + 1) * capacity]


def norm_kernel(ctx_count, part_count, gain_ref, place_ref, route_ref, next_ref, *refs):
    part_refs = refs[:part_count]
    residual_ref, normed_ref, *out_refs = refs[-2 - ctx_count :]
    columns = residual_ref.shape[2]
    total = merged(part_refs[0][...])
    for part_ref in part_refs[1:]:
        total = total + merged(part_ref[...]).astype(jnp.float32)
    residual = total.astype(jnp.bfloat16)
    residual_ref[...] = residual.reshape(residual_ref.shape)
    res_float = residual.astype(jnp.float32)
    mean = jnp.mean(res_float * res_float, axis=-1, keepdims=True)
    normed = (res_float * lax.rsqrt(mean + 1e-05) * gain_ref[...]).astype(jnp.bfloat16)
    put_slots(place_ref, normed, out_refs)
    route = route_ref[...] + next_ref[...]
    normed_ref[:, :, :columns] = normed.reshape(residual_ref.shape)
    normed_ref[:, :, columns:] = route.reshape(normed_ref.shape[:2] + route.shape[1:])


def norm_and_pick(gain, place, route, following, parts, ctx_count, after):
    _, half, columns = parts[0].shape
    slot = jax.ShapeDtypeStruct((place.shape[0] // ctx_count, columns), jnp.bfloat16)
    return pl.pallas_call(
        functools.partial(norm_kernel, ctx_count, len(parts)),
        out_shape=[
            jax.ShapeDtypeStruct((2, half, columns), jnp.bfloat16),
            jax.ShapeDtypeStruct((2, half, columns + route.shape[1]), jnp.bfloat16),
        ]
        + [slot] * ctx_count,
        in_specs=[VMEM_SPEC] * (4 + len(parts)) + [ANY_SPEC] * len(after),
        out_specs=[VMEM_SPEC] * (2 + ctx_count),
        compiler_params=pltpu.CompilerParams(vmem_limit_bytes=12 << 20),
        cost_estimate=SMALL_COST,
    )(gain, place, route, following, *parts, *after)


def pick_kernel(ctx_count, place_ref, held_ref, *refs):
    out_refs = refs[-ctx_count:]
    put_slots(place_ref, merged(held_ref[:, :, : out_refs[0].shape[1]]), out_refs)


def pick_rows(place, held, like, after):
    ctx_count = len(like)
    return pl.pallas_call(
        functools.partial(pick_kernel, ctx_count),
        out_shape=[jax.ShapeDtypeStruct(like[0].shape, like[0].dtype)] * ctx_count,
        in_specs=[VMEM_SPEC] * 2 + [ANY_SPEC] * len(after),
        out_specs=[VMEM_SPEC] * ctx_count,
        compiler_params=pltpu.CompilerParams(vmem_limit_bytes=6 << 20),
        cost_estimate=SMALL_COST,
    )(place, held, *after)


def expert_kernel(ctx_count, tile, *refs):
    row_refs, refs = refs[:ctx_count], refs[ctx_count:]
    gate_up_refs, down_refs = refs[:2], refs[2:4]
    out_refs, total_ref = refs[-ctx_count - 1 : -1], refs[-1]
    capacity = row_refs[0].shape[0]

    def add_tile(i, carry):
        routed = jnp.concatenate([row_ref[...] for row_ref in row_refs], axis=0)
        here = pl.ds(pl.multiple_of(i * tile, tile), tile)
        added = None
        for gate_up_ref, down_ref in zip(gate_up_refs, down_refs):
            gate = nt_dot(routed, gate_up_ref[0, here])
            up = nt_dot(routed, gate_up_ref[1, here])
            activated = gate * jax.nn.sigmoid(1.702 * gate) * (up + 1.0)
            term = nn_dot(activated.astype(jnp.bfloat16), down_ref[here])
            added = term if added is None else added + term

        @pl.when(i == 0)
        def _():
            total_ref[...] = added

        @pl.when(i > 0)
        def _():
            total_ref[...] += added

        return carry

    lax.fori_loop(0, down_refs[0].shape[0] // tile, add_tile, 0)
    for d, out_ref in enumerate(out_refs):
        out_ref[...] = total_ref[d * capacity : (d + 1) * capacity].astype(jnp.bfloat16)


def expert(rows, gate_ups, downs, after, tiles):
    ctx_count = len(rows)
    capacity, columns = rows[0].shape
    tile = downs[0].shape[0] // tiles
    return pl.pallas_call(
        functools.partial(expert_kernel, ctx_count, tile),
        out_shape=[jax.ShapeDtypeStruct((capacity, columns), jnp.bfloat16)] * ctx_count,
        in_specs=[VMEM_SPEC] * (ctx_count + 4) + [ANY_SPEC] * len(after),
        out_specs=[VMEM_SPEC] * ctx_count,
        scratch_shapes=[pltpu.VMEM((ctx_count * capacity, columns), jnp.float32)],
        compiler_params=pltpu.CompilerParams(vmem_limit_bytes=16 << 20),
        cost_estimate=SMALL_COST,
    )(*rows, *gate_ups, *downs, *after)


def mix_kernel(ctx_count, extra_count, mix_ref, *refs):
    back_refs, extra_refs = refs[:ctx_count], refs[ctx_count : ctx_count + extra_count]
    out_ref = refs[-1]
    back = jnp.concatenate([back_ref[...] for back_ref in back_refs], axis=0)
    total = nn_dot(mix_ref[...], back)
    for extra_ref in extra_refs:
        total = total + merged(extra_ref[...]).astype(jnp.float32)
    out_ref[...] = total.astype(out_ref.dtype).reshape(out_ref.shape)


def mix_rows(mix, back, extra, after, dtype=jnp.bfloat16):
    tokens, count = mix.shape
    columns = back[0].shape[1]
    shape = (2, tokens // 2, columns)
    return pl.pallas_call(
        functools.partial(mix_kernel, len(back), len(extra)),
        out_shape=jax.ShapeDtypeStruct(shape, dtype),
        in_specs=[VMEM_SPEC] * (1 + len(back) + len(extra)) + [ANY_SPEC] * len(after),
        out_specs=VMEM_SPEC,
        compiler_params=pltpu.CompilerParams(vmem_limit_bytes=8 << 20),
        cost_estimate=SMALL_COST,
    )(mix, *back, *extra, *after)


def sum_kernel(part_count, *refs):
    total = refs[0][...]
    for part_ref in refs[1:part_count]:
        total = total + part_ref[...].astype(jnp.float32)
    refs[-1][...] = total.astype(jnp.bfloat16)


def sum_parts(parts, after):
    return pl.pallas_call(
        functools.partial(sum_kernel, len(parts)),
        out_shape=jax.ShapeDtypeStruct(parts[0].shape, jnp.bfloat16),
        in_specs=[VMEM_SPEC] * len(parts) + [ANY_SPEC] * len(after),
        out_specs=VMEM_SPEC,
        compiler_params=pltpu.CompilerParams(vmem_limit_bytes=4 << 20),
        cost_estimate=SMALL_COST,
    )(*parts, *after)


def local(
    queries,
    key_rows,
    value_matrix,
    hidden,
    out_weight,
    norm_gain,
    block_order,
    expert_ids,
    route_weights,
    gate_up_weight,
    down_weight,
):
    ctx_count = lax.axis_size("ctx")
    planes = lax.axis_size("exp") // 2
    ctx_scalar = lax.axis_index("ctx").astype(jnp.int32).reshape(1)
    plane_index = (lax.axis_index("exp") // 2).astype(jnp.int32)
    token_count = queries.shape[1]
    experts = ctx_count * planes
    capacity = 2 * token_count * TOPK // experts
    last = ctx_count - 1
    plane_scalars = jnp.stack(
        [plane_index, jnp.full_like(plane_index, planes), jnp.full_like(plane_index, capacity)]
    )

    route = jnp.concatenate(
        [expert_ids[0].astype(jnp.bfloat16), route_weights[0].astype(jnp.bfloat16)], axis=1
    )
    spare = -D % 128
    following = jnp.pad(route, ((0, 0), (2 * TOPK, spare - 4 * TOPK)))
    route = jnp.pad(route, ((0, 0), (0, spare - 2 * TOPK)))
    mask_shape = (token_count, ctx_count * capacity)

    packed = pack(ctx_scalar, queries[0], key_rows[0], value_matrix[0], ctx_count)
    got = [ctx_swap(packed[d], d) for d in range(ctx_count)]

    gate_up_mine = jnp.swapaxes(gate_up_weight[0], 0, 1)
    down_mine = down_weight[0]
    half = down_mine.shape[0]
    got, gate_up_mine, down_mine = lax.optimization_barrier((got, gate_up_mine, down_mine))

    weight = jnp.swapaxes(out_weight, 0, 1)
    first = list(attend((last,), ctx_scalar, block_order, weight, got, [], []))
    partners = tuple(range(last - 1, 0, -1))
    parts = list(attend(partners, ctx_scalar, block_order, weight, got, [], first))
    swapped = [core_swap(gate_up_mine), core_swap(down_mine)]
    hidden_columns = jnp.swapaxes(hidden[0], 0, 1)
    added = [hidden_columns, ctx_swap(first[0], last)]
    own = attend((0,), ctx_scalar, block_order, weight, got, added, parts[:1])
    parts = [ctx_swap(part, partners[i]) for i, part in enumerate(parts)]
    following, _ = lax.optimization_barrier((following, added[1]))
    following = plane_shift(following, 1)
    mix, place, next_mix, next_place = masks(
        ctx_scalar, plane_scalars, [route, following], (0, 2 * TOPK), *mask_shape
    )
    other = [copy_after(w, list(own)) for w in swapped]
    gate_ups = [w.reshape(2, half, D) for w in (gate_up_mine, other[0])]
    downs = [down_mine, other[1]]

    residual, held, *rows = norm_and_pick(
        norm_gain[None], place, route, following, list(own) + parts, ctx_count, other
    )

    def spread(blocks):
        return [ctx_swap(blocks[d], d) for d in range(ctx_count)]

    mixes = [mix]
    arrived = [spread(rows)]
    back = [None] * planes

    def run_expert(s, after):
        result = expert(arrived[s], gate_ups, downs, after, 1 if s == planes - 1 else 3)
        if s > 0:
            back[s] = spread(result)
        return list(result)

    def run_mix(s, carried, after):
        part = mix_rows(mixes[s], back[s], carried, after)
        return [part], [plane_shift(part, 1)]

    done, carried = [], []
    for s in range(1, planes):
        held = plane_shift(held, 1)
        mixes.append(next_mix)
        rows = pick_rows(next_place, held, rows, arrived[s - 1][1:] + done[:1])
        held, rows = lax.optimization_barrier((held, rows))
        arrived.append(spread(rows))
        after = list(rows[:1])
        if s < planes - 1:
            next_mix, next_place = masks(
                ctx_scalar, plane_scalars, [held], (2 * TOPK,), *mask_shape
            )
            after.append(next_mix)
        done = run_expert(s - 1, after)
        if s == 1:
            own_result = done
        if s > 2:
            done, carried = run_mix(s - 2, carried, done)
    done = run_expert(planes - 1, done)
    own_result, _ = lax.optimization_barrier((own_result, done))
    back[0] = spread(own_result)
    for s in range(max(planes - 2, 1), planes):
        done, carried = run_mix(s, carried, done)
    own = mix_rows(mixes[0], back[0], [residual], done, jnp.float32)
    out = sum_parts([own] + carried, [])
    return out.reshape(1, token_count, D)


def solution(mesh):
    return jax.shard_map(
        local,
        mesh=mesh,
        in_specs=(
            P("exp", "ctx", None),
            P("exp", "ctx", None),
            P("exp", "ctx", None),
            P("exp", "ctx", None),
            P("ctx", None),
            P(),
            P(),
            P("exp", "ctx", None),
            P("exp", "ctx", None),
            P(("ctx", "exp"), None, None),
            P(("ctx", "exp"), None, None),
        ),
        out_specs=P("exp", "ctx", None),
        check_vma=False,
    )
```
